128 devices in a mesh: ray: 4 (over y), region: 32 (over z, x, core).
Axes of the slice: x: 4, y: 4, z: 4, core: 2. Of those that a mesh axis runs over, the one named last changes fastest.
Arguments:
- features: bfloat16 [8192, 128, 256], P(('ray', 'region')), may hold values from -6 to 6
- deltas: bfloat16 [8192, 128], P(('ray', 'region')), may hold values from 0.0005 to 0.06
- weight_one: bfloat16 [32, 256, 256], P('region'), may hold values from -0.375 to 0.375
- weight_two: bfloat16 [32, 256, 256], P('region'), may hold values from -0.375 to 0.375
- weight_out: bfloat16 [32, 256, 4], P('region'), may hold values from -0.375 to 0.375
- target: float32 [2048, 3], P(('ray', 'region')), may hold values from 0 to 1
- block_region: int32 [8192, 1], P(('ray', 'region')), may hold values from 0 to 31; in each aligned block of 64 rows (0 to 63, 64 to 127, ...) at most 4 rows name the same one
- seg_order: int32 [2048, 4], P(('ray', 'region')), may hold values from 0 to 3, each once within a row
- owner_map: int32 [32], replicated, may hold values from 0 to 31, each once
Outputs:
- ray_color: float32 [2048, 3], P(('ray', 'region'))
- grad_one: float32 [32, 256, 256], P('region')
- grad_two: float32 [32, 256, 256], P('region')
- grad_out: float32 [32, 256, 4], P('region')
The draws below stay inside these ranges and needn't reach their ends.
Inputs may be any that keep to these rules, and one draw needn't show every extreme that they name: `block_region`: among the 64 blocks of one device no region appears more than 4 times, and some region appears exactly 4 times. `seg_order`: each row is a permutation of 0 .. 3. `owner_map`: A permutation of 0 .. 31.
All inputs are finite; a program needn't handle non-finite values.
Results may differ from the reference program's by a relative error of at most 0.0095.
The reference program's roundings to bfloat16 on the way (of `hidden_one`, `hidden_two`, `d_raw`, `d_two` and `d_one`) count: a program that leaves them out, or rounds other values in their place, can miss the bound.
Values may be sent and summed in bfloat16 or wider, within the bound.
No kernel may reach another device: no remote copies, remote signals or barrier semaphores. Data moves between devices by JAX's collectives and lax.ppermute only.
A program may use at most 128 MiB of HBM per device.

```python
import math
import jax
import jax.numpy as jnp
import numpy as np
from jax import lax

D = 256
SAMP = 128
SEG = 4
BLK_DEV = 64
REGIONS = 32
MOST = 4
BLOCKS = 8192
RAYS = 2048


def draw_deltas(key, part):
    key = jax.random.fold_in(key, 11)
    block_key, sample_key = jax.random.split(key)
    block_scale = jnp.exp(jax.random.uniform(block_key, (BLOCKS, 1), jnp.float32, math.log(0.001), math.log(0.03)))
    jitter = jnp.exp(jax.random.uniform(sample_key, (BLOCKS, SAMP), jnp.float32, math.log(0.5), math.log(2.0)))
    return (block_scale * jitter).astype(jnp.bfloat16)


def block_levels(own_key, shape, cuts, least, top_value):
    factor_of = 1.0
    for dim, shards_of in cuts:
        steps = jax.random.uniform(jax.random.fold_in(jax.random.fold_in(own_key, 6), dim), (shards_of,), jnp.float32, least / len(cuts), top_value / len(cuts))
        factor_of = factor_of * jnp.repeat(jnp.exp(steps), shape[dim] // shards_of).reshape((-1,) + (1,) * (len(shape) - 1 - dim))
    return factor_of


def shared_out(key, own, number, rows, number_of, top, most, lean):
    order = jax.random.permutation(key, number_of)
    heavy_load, ordinary = portions_of(number_of, rows * top, most, lean, True), portions_of(number_of, rows * top, most, lean, False)
    places = jnp.arange(number_of)

    def named(lengths, rotation):
        used = int((lengths > 0).sum())
        fixed = max(1, used // 4)
        moved = fixed + (places - fixed + rotation * (used - fixed)) % max(1, number_of - fixed)
        return jnp.zeros((number_of,), jnp.int32).at[order[jnp.where(places < fixed, places, moved)]].set(jnp.asarray(lengths, jnp.int32))

    lengths = jnp.where(number % 4 == 0, named(heavy_load, number // 4), named(ordinary, number - number // 4 - 1))
    mixed = jax.random.permutation(jax.random.fold_in(own, 3), number_of)
    source_of, receiver = mixed[0:number_of // 2 * 2:2], mixed[1:number_of // 2 * 2:2]
    room = jnp.minimum(lengths[source_of] - 1, most - lengths[receiver]) // 2
    room = jnp.where((source_of == order[0]) | (receiver == order[0]) | (lengths[receiver] == 0), 0, jnp.maximum(room, 0))
    moved = jax.random.randint(jax.random.fold_in(own, 4), (number_of // 2,), 0, 1 << 20) % (room + 1)
    lengths = lengths.at[source_of].add(-moved).at[receiver].add(moved)
    members = jnp.searchsorted(jnp.cumsum(lengths), jnp.arange(rows * top), side="right").astype(jnp.int32)
    listing = members.reshape(top, rows).T
    listing = listing[jax.random.permutation(jax.random.fold_in(own, 1), rows)]
    rotation = jax.random.randint(jax.random.fold_in(own, 2), (rows, 1), 0, top)
    return jnp.take_along_axis(listing, (jnp.arange(top)[None, :] + rotation) % top, axis=1)


def portions_of(amount, total, limit, lean, full):
    loads = [(1 << 20) // math.isqrt(rank ** lean) + 1 for rank in range(1, amount + 1)]
    largest = limit if full else min(limit, max(-(-total // amount), total * loads[0] // sum(loads)))
    least = 1 if total - largest >= amount - 1 else 0
    holding, spare = [largest] + [least] * (amount - 1), total - largest - least * (amount - 1)
    while spare > 0:
        candidates = [i for i in range(1, amount) if holding[i] < largest] or [i for i in range(1, amount) if holding[i] < limit]
        pool, remaining = sum([loads[i] for i in candidates]), spare
        for i in candidates:
            extra = min(limit - holding[i], max(1, remaining * loads[i] // pool), spare)
            holding[i] = holding[i] + extra
            spare = spare - extra
    return np.array(holding)


def centred(own_key, extent, deviation, most, pieces=(), kind=jnp.bfloat16):
    drawn = jax.random.normal(own_key, extent, jnp.float32) * deviation
    if len(pieces) > 0:
        drawn = block_levels(own_key, extent, pieces, -0.22, 0.18) * drawn
    return jnp.clip(drawn, min=-most, max=most).astype(kind)


def setup_inputs(seed: int = 0) -> dict:
    key_of = jax.random.split(jax.random.key(seed), 10)
    features = centred(key_of[0], (BLOCKS, SAMP, D), 1.0, 6.0, ((0, 128),))
    deltas = draw_deltas(jax.random.fold_in(key_of[9], 71), 0)
    weight_one = centred(key_of[2], (REGIONS, D, D), D ** -0.5, 0.375, ((0, 32),))
    weight_two = centred(key_of[3], (REGIONS, D, D), D ** -0.5, 0.375, ((0, 32),))
    weight_out = centred(key_of[4], (REGIONS, D, 4), D ** -0.5, 0.375, ((0, 32),))
    target = jnp.clip(1.0 * jax.random.uniform(key_of[5], (RAYS, 3), jnp.float32) ** block_levels(key_of[5], (RAYS, 3), ((0, 128),), -0.2, 0.2), 0.0, 1.0)
    block_region_keys = jax.random.split(jax.random.fold_in(key_of[6], 1), BLOCKS // BLK_DEV)
    block_region_turns = jax.random.permutation(jax.random.fold_in(key_of[6], 3), BLOCKS // BLK_DEV)
    block_region = jax.vmap(lambda own, number: shared_out(jax.random.fold_in(key_of[6], 2), own, number, BLK_DEV, REGIONS, 1, MOST, 2))(block_region_keys, block_region_turns).reshape((BLOCKS, 1))
    seg_order = jax.vmap(lambda own: jax.random.permutation(own, SEG))(jax.random.split(key_of[7], RAYS)).reshape((RAYS, SEG)).astype(jnp.int32)
    owner_map = jax.random.permutation(key_of[8], REGIONS).astype(jnp.int32)
    return {"features": features, "deltas": deltas, "weight_one": weight_one, "weight_two": weight_two, "weight_out": weight_out, "target": target, "block_region": block_region, "seg_order": seg_order, "owner_map": owner_map}


def shade(x, delta, w_one, w_two, w_head):
    f32 = jnp.float32
    pre_one = jnp.einsum("agbpd,gde->agbpe", x.astype(f32), w_one.astype(f32))
    hidden_one = jax.nn.relu(pre_one).astype(jnp.bfloat16)
    pre_two = jnp.einsum("agbpd,gde->agbpe", hidden_one.astype(f32), w_two.astype(f32))
    hidden_two = jax.nn.relu(pre_two).astype(jnp.bfloat16)
    raw = jnp.einsum("agbpd,gdk->agbkp", hidden_two.astype(f32), w_head.astype(f32))
    sigma = jax.nn.softplus(raw[..., 0, :])
    rgb = jax.nn.sigmoid(raw[..., 1:, :])
    tau = sigma * delta.astype(f32)
    transmittance = jnp.exp(-(jnp.cumsum(tau, -1) - tau))
    opacity_value = 1.0 - jnp.exp(-tau)
    weight = transmittance * opacity_value
    color = jnp.sum(weight[..., None, :] * rgb, -1)
    log_trans = -jnp.sum(tau, -1)
    result = jnp.concatenate([color, log_trans[..., None]], -1)
    return result, (pre_one, hidden_one, pre_two, hidden_two, raw, rgb, transmittance, opacity_value, weight)


def unshade(x, delta, w_one, w_two, w_head, saved, output_gradient):
    f32 = jnp.float32
    pre_one, hidden_one, pre_two, hidden_two, raw, rgb, transmittance, opacity_value, weight = saved
    color_gradient = output_gradient[..., :3]
    log_transmittance_gradient = output_gradient[..., 3]
    d_rgb = weight[..., None, :] * color_gradient[..., None]
    weight_gradient = jnp.sum(rgb * color_gradient[..., None], -2)
    prod = weight_gradient * weight
    following_segments = jnp.sum(prod, -1, keepdims=True) - jnp.cumsum(prod, -1)
    optical_depth_gradient = -log_transmittance_gradient[..., None] + weight_gradient * transmittance * (1.0 - opacity_value) - following_segments
    d_sig = optical_depth_gradient * delta.astype(f32) * jax.nn.sigmoid(raw[..., 0, :])
    d_col = d_rgb * rgb * (1.0 - rgb)
    d_raw = jnp.concatenate([d_sig[..., None, :], d_col], -2).astype(jnp.bfloat16)
    g_head = jnp.einsum("agbpd,agbkp->gdk", hidden_two.astype(f32), d_raw.astype(f32))
    dh_two = jnp.einsum("agbkp,gdk->agbpd", d_raw.astype(f32), w_head.astype(f32))
    d_two = jnp.where(pre_two > 0, dh_two, 0.0).astype(jnp.bfloat16)
    g_two = jnp.einsum("agbpd,agbpe->gde", hidden_one.astype(f32), d_two.astype(f32))
    dh_one = jnp.einsum("agbpe,gde->agbpd", d_two.astype(f32), w_two.astype(f32))
    d_one = jnp.where(pre_one > 0, dh_one, 0.0).astype(jnp.bfloat16)
    g_one = jnp.einsum("agbpd,agbpe->gde", x.astype(f32), d_one.astype(f32))
    return g_one, g_two, g_head


def composite(results, seg_order, target):
    seg = seg_order.shape[1]
    parts = results.reshape(-1, seg, 4)
    colors = parts[..., :3]
    log_trans = parts[..., 3]
    prior_transmittance = (seg_order[:, None, :] < seg_order[:, :, None]).astype(jnp.float32)
    reach = jnp.exp(jnp.sum(prior_transmittance * log_trans[:, None, :], -1))
    color = jnp.sum(reach[..., None] * colors, 1)
    gray = color - target
    color_gradient = reach[..., None] * gray[:, None, :]
    segment_portion = reach * jnp.sum(colors * gray[:, None, :], -1)
    log_transmittance_gradient = jnp.sum(prior_transmittance * segment_portion[:, :, None], 1)
    output_gradient = jnp.concatenate([color_gradient, log_transmittance_gradient[..., None]], -1).reshape(-1, 4)
    return color, output_gradient


def reference(features, deltas, weight_one, weight_two, weight_out, target, block_region, seg_order, owner_map):
    slots = owner_map[block_region[:, 0]].astype(jnp.int32)
    group = 8
    xs = features.reshape(BLOCKS // group, group, SAMP, D)
    ds = deltas.reshape(BLOCKS // group, group, SAMP)
    ss = slots.reshape(BLOCKS // group, group)

    def forward(item):
        x, d, s = item
        res, _ = shade(x[None, :, None], d[None, :, None], weight_one[s], weight_two[s], weight_out[s])
        return res[0, :, 0]

    results = lax.map(forward, (xs, ds, ss)).reshape(BLOCKS, 4)
    color, output_gradient = composite(results, seg_order, target)
    cs = output_gradient.reshape(BLOCKS // group, group, 4)

    def backward(carry, item):
        x, d, s, c = item
        w1, w2, wo = weight_one[s], weight_two[s], weight_out[s]
        _, saved = shade(x[None, :, None], d[None, :, None], w1, w2, wo)
        g1, g2, go = unshade(x[None, :, None], d[None, :, None], w1, w2, wo, saved, c[None, :, None])
        return (carry[0].at[s].add(g1), carry[1].at[s].add(g2), carry[2].at[s].add(go)), None

    init = (jnp.zeros((REGIONS, D, D), jnp.float32), jnp.zeros((REGIONS, D, D), jnp.float32), jnp.zeros((REGIONS, D, 4), jnp.float32))
    grads, _ = lax.scan(backward, init, (xs, ds, ss, cs))
    return color, grads[0], grads[1], grads[2]
```

```python
import functools

import jax
import jax.numpy as jnp
from jax import lax
from jax.experimental import pallas as pl
from jax.experimental.pallas import tpu as pltpu
from jax.sharding import PartitionSpec as P

F32, BF16, I32 = jnp.float32, jnp.bfloat16, jnp.int32
NS = 16
NP = 64
ROWS = 528
VMEM = pltpu.CompilerParams(vmem_limit_bytes=56 * 1024 * 1024)
HI = lax.Precision.HIGHEST

TREE = (
    ((0, 1), (0, 0), "x", 1),
    ((0, 3), (0, 0), "x", 3),
    ((1, 0), (0, 0), "z", 1),
    ((3, 0), (0, 0), "z", 3),
    ((0, 2), (0, 1), "x", 1),
    ((1, 3), (1, 0), "x", 3),
    ((2, 0), (1, 0), "z", 1),
    ((3, 3), (0, 3), "z", 3),
    ((1, 1), (1, 0), "x", 1),
    ((3, 1), (0, 1), "z", 3),
    ((1, 2), (0, 2), "z", 1),
    ((3, 2), (3, 3), "x", 3),
    ((2, 1), (2, 0), "x", 1),
    ((2, 3), (2, 0), "x", 3),
    ((2, 2), (1, 2), "z", 1),
)


def move(axis, step):
    pairs = []
    for z in range(4):
        for x in range(4):
            for c in range(2):
                z2, x2, c2 = z, x, c
                if axis == "z":
                    z2 = (z + step) % 4
                elif axis == "x":
                    x2 = (x + step) % 4
                else:
                    c2 = 1 - c
                pairs.append((z * 8 + x * 2 + c, z2 * 8 + x2 * 2 + c2))
    return pairs


def iota(shape, dim):
    return lax.broadcasted_iota(I32, shape, dim)


def meta_kernel(place, owner, region, order, target, out):
    spot = region[...]
    slot = jnp.zeros((64, 1), I32)
    for r in range(32):
        slot = jnp.where(spot == r, owner[r], slot)
    dz = ((slot >> 3) - place[0]) & 3
    dx = (((slot >> 1) & 3) - place[1]) & 3
    key = (dz * 4 + dx) * 2 + (slot & 1)
    eye = iota((64, 128), 0) == iota((64, 128), 1)
    key_row = jnp.sum(jnp.where(eye, key.astype(F32), 0.0), 0, keepdims=True)
    lane = iota((16, 128), 1)
    mine = (lane >> 2) == iota((16, 128), 0)
    seg = order[...].astype(F32)
    spread = jnp.zeros((16, 128), F32)
    for k in range(4):
        spread = jnp.where((lane & 3) == k, seg[:, k : k + 1], spread)
    rows = [key_row, jnp.sum(jnp.where(mine, spread, 0.0), 0, keepdims=True)]
    for c in range(3):
        rows.append(jnp.sum(jnp.where(mine, target[:, c : c + 1], 0.0), 0, keepdims=True))
    rows.append(jnp.zeros((3, 128), F32))
    out[...] = jnp.concatenate(rows, 0)


def both(a, b):
    lane = iota(a.shape, 1)
    return jnp.where(lane < 64, a, pltpu.roll(b, 64, 1))


def plan_kernel(place, own, sib, table, code_out):
    meta = both(own[...], sib[...])
    key = meta[0:1].astype(I32)
    rel, valid = key >> 1, (key & 1) == place[2]
    hot = (iota((NS, 128), 0) == rel) & valid
    hotf = jnp.where(hot, 1.0, 0.0)
    before = jnp.where(iota((128, 128), 0) < iota((128, 128), 1), 1.0, 0.0)
    cum = jnp.dot(hotf, before, preferred_element_type=F32)
    rank = jnp.sum(hotf * cum, 0, keepdims=True).astype(I32)
    count = jnp.sum(hotf, 1, keepdims=True).astype(I32)
    pairs = ((count + 1) >> 1).astype(F32)
    eye = iota((NS, 128), 0) == iota((NS, 128), 1)
    pairs_row = jnp.sum(jnp.where(eye, pairs, 0.0), 0, keepdims=True)
    ahead = iota((NS, 128), 1) < iota((NS, 128), 0)
    start = jnp.sum(jnp.where(ahead, pairs_row, 0.0), 1, keepdims=True)
    start_row = jnp.sum(jnp.where(eye, start, 0.0), 0, keepdims=True)
    start_j = jnp.sum(hotf * start, 0, keepdims=True).astype(I32)
    code = start_j + (rank >> 1) + (rank & 1) * NP
    code = jnp.where(valid, code, -1)
    square = iota((128, 128), 0) == iota((128, 128), 1)
    code_col = jnp.sum(jnp.where(square, code.astype(F32), 0.0), 1, keepdims=True)
    source = (iota((128, 128), 0) + 1).astype(F32)
    hit = code_col.astype(I32) == iota((128, 128), 1)
    inverse = jnp.sum(jnp.where(hit, source, 0.0), 0, keepdims=True).astype(I32) - 1
    begun = jnp.where(start.astype(I32) <= iota((NS, 128), 1), 1.0, 0.0)
    slot_of = jnp.sum(begun, 0, keepdims=True).astype(I32) - 1
    total = jnp.sum(pairs_row, 1, keepdims=True).astype(I32)
    table[...] = jnp.concatenate(
        [
            inverse,
            slot_of,
            start_row.astype(I32),
            pairs_row.astype(I32),
            jnp.broadcast_to(total, (1, 128)),
            jnp.zeros((3, 128), I32),
        ],
        0,
    )
    code_out[...] = jnp.broadcast_to(code, (8, 128))


def fetch(table, own, sib, xs, sems, pairs):
    def one(i, h):
        src = table[0, h * NP + i]

        @pl.when(src < 0)
        def _():
            xs[i, h] = jnp.zeros((128, 256), BF16)

        @pl.when((src >= 0) & (src < 64))
        def _():
            pltpu.make_async_copy(own.at[src], xs.at[i, h], sems.at[i, h]).start()

        @pl.when(src >= 64)
        def _():
            pltpu.make_async_copy(sib.at[src - 64], xs.at[i, h], sems.at[i, h]).start()

    def step(i, _):
        one(i, 0)
        one(i, 1)
        return 0

    lax.fori_loop(0, pairs, step, 0)


def arrive(table, own, xs, sems, i):
    for h in range(2):

        @pl.when(table[0, h * NP + i] >= 0)
        def _():
            pltpu.make_async_copy(own.at[0], xs.at[i, h], sems.at[i, h]).wait()


def forward_kernel(*refs):
    table, code, own, sib, d_own, d_sib = refs[:6]
    weights = refs[6 : 6 + NS]
    res, saved, h1_out, h2_out = refs[6 + NS : 10 + NS]
    xs, wv, h1, h2, raw, xsem, wsem, hsem = refs[10 + NS :]
    total = table[4, 0]
    even = (total + 1) // 2 * 2
    for s in range(NS):
        pltpu.make_async_copy(weights[s], wv.at[s], wsem.at[s]).start()
    fetch(table, own, sib, xs, xsem, even)
    raw[...] = jnp.zeros(raw.shape, F32)
    for s in range(NS):
        pltpu.make_async_copy(weights[s], wv.at[s], wsem.at[s]).wait()

    def shade(i):
        slot = table[1, i]
        arrive(table, own, xs, xsem, i)
        x = xs[i].reshape(256, 256)
        pre = jnp.dot(x, wv[slot, 0:256], preferred_element_type=F32)
        one = jnp.maximum(pre, 0.0).astype(BF16)
        h1[i] = one
        pre = jnp.dot(one, wv[slot, 256:512], preferred_element_type=F32)
        two = jnp.maximum(pre, 0.0).astype(BF16)
        h2[i] = two
        out = lax.dot_general(
            wv[slot, 512:528], two, (((1,), (1,)), ((), ())), preferred_element_type=F32
        )
        rows = pl.ds(pl.multiple_of(i * 8, 8), 8)
        raw[0, rows, :] = out[0:8, 0:128]
        raw[1, rows, :] = out[0:8, 128:256]
        pltpu.make_async_copy(h1.at[i], h1_out.at[i], hsem.at[0, i]).start()
        pltpu.make_async_copy(h2.at[i], h2_out.at[i], hsem.at[1, i]).start()

    def step(t, _):
        shade(2 * t)
        shade(2 * t + 1)
        return 0

    lax.fori_loop(0, even // 2, step, 0)

    before = jnp.where(iota((128, 128), 0) < iota((128, 128), 1), 1.0, 0.0)
    spot = code[0:1]
    out = jnp.zeros((4, 128), F32)
    for h in range(2):
        lanes = slice(h * 128, h * 128 + 128)
        pick = spot == iota((NP, 128), 0) + h * NP
        pickb = jnp.where(pick, 1.0, 0.0).astype(BF16)
        deltas = jnp.concatenate([d_own[...], d_sib[...]], 0)
        delta = jnp.dot(pickb, deltas, preferred_element_type=F32)
        ch = [raw[h, pl.ds(c, NP, stride=8), :] for c in range(4)]
        sigma = jnp.maximum(ch[0], 0.0) + jnp.log1p(jnp.exp(-jnp.abs(ch[0])))
        rgb = [jax.nn.sigmoid(ch[c]) for c in (1, 2, 3)]
        tau = sigma * delta
        cum = jnp.dot(tau, before, precision=HI, preferred_element_type=F32)
        trans = jnp.exp(-cum)
        opacity = 1.0 - jnp.exp(-tau)
        weight = trans * opacity
        cols = [jnp.sum(weight * rgb[c], 1, keepdims=True) for c in range(3)]
        cols.append(-jnp.sum(tau, 1, keepdims=True))
        out += jnp.concatenate(
            [jnp.sum(jnp.where(pick, col, 0.0), 0, keepdims=True) for col in cols], 0
        )
        keep = rgb + [weight, trans * (1.0 - opacity), delta * jax.nn.sigmoid(ch[0])]
        for k in range(6):
            saved[k, :, lanes] = keep[k]
    res[...] = jnp.concatenate([out, jnp.zeros((4, 128), F32)], 0)

    def drain(i, _):
        pltpu.make_async_copy(h1.at[i], h1_out.at[i], hsem.at[0, i]).wait()
        pltpu.make_async_copy(h2.at[i], h2_out.at[i], hsem.at[1, i]).wait()
        return 0

    lax.fori_loop(0, even, drain, 0)


def backward_kernel(*refs):
    table, code, own, sib, res, res_sib, m_own, m_sib, saved, h1_in, h2_in = refs[:11]
    weights = refs[11 : 11 + NS]
    color_out = refs[11 + NS]
    grads = refs[12 + NS : 12 + 2 * NS]
    xs, wv, h1, h2, dr, acc1, acc2, acc3, stage, xsem, wsem, hsem, gsem = refs[12 + 2 * NS :]
    total = table[4, 0]
    for s in range(NS):
        pltpu.make_async_copy(weights[s].at[pl.ds(256, 272)], wv.at[s], wsem.at[s]).start()

    def load(i, _):
        pltpu.make_async_copy(h1_in.at[i], h1.at[i], hsem.at[0, i]).start()
        pltpu.make_async_copy(h2_in.at[i], h2.at[i], hsem.at[1, i]).start()
        return 0

    lax.fori_loop(0, total, load, 0)
    fetch(table, own, sib, xs, xsem, total)

    meta = both(m_own[...], m_sib[...])
    parts = res[...] + pltpu.roll(res_sib[...], 64, 1)
    order = meta[1:2]
    square = (128, 128)
    same = (iota(square, 0) >> 2) == (iota(square, 1) >> 2)
    samef = jnp.where(same, 1.0, 0.0)
    eye = iota(square, 0) == iota(square, 1)
    order_col = jnp.sum(jnp.where(eye, order, 0.0), 1, keepdims=True)
    prior = jnp.where(same & (order_col < order), 1.0, 0.0)
    later = jnp.where(same & (order_col > order), 1.0, 0.0)
    ahead = jnp.dot(parts, prior, precision=HI, preferred_element_type=F32)[3:4]
    reach = jnp.exp(ahead)
    shown = parts * reach
    color = jnp.dot(shown, samef, precision=HI, preferred_element_type=F32)
    color_out[...] = color
    gray = color[0:3] - meta[2:5]
    portion = jnp.sum(shown[0:3] * gray, 0, keepdims=True)
    log_cot = jnp.dot(
        jnp.broadcast_to(portion, (8, 128)), later, precision=HI, preferred_element_type=F32
    )[0:1]
    cot = [reach * gray[c : c + 1] for c in range(3)] + [log_cot]

    after = jnp.where(iota(square, 0) > iota(square, 1), 1.0, 0.0)
    spot = code[0:1]
    dr[...] = jnp.zeros(dr.shape, F32)
    for h in range(2):
        lanes = slice(h * 128, h * 128 + 128)
        pick = spot == iota((NP, 128), 0) + h * NP
        col = [jnp.sum(jnp.where(pick, row, 0.0), 1, keepdims=True) for row in cot]
        rgb = [saved[c, :, lanes] for c in range(3)]
        weight = saved[3, :, lanes]
        d_weight = rgb[0] * col[0] + rgb[1] * col[1] + rgb[2] * col[2]
        follow = jnp.dot(d_weight * weight, after, precision=HI, preferred_element_type=F32)
        d_tau = d_weight * saved[4, :, lanes] - col[3] - follow
        dr[h, pl.ds(0, NP, stride=8), :] = d_tau * saved[5, :, lanes]
        for c in range(3):
            d_col = weight * col[c] * rgb[c] * (1.0 - rgb[c])
            dr[h, pl.ds(c + 1, NP, stride=8), :] = d_col

    for s in range(NS):
        pltpu.make_async_copy(weights[s].at[pl.ds(256, 272)], wv.at[s], wsem.at[s]).wait()

    for s in range(NS):
        begin, count = table[2, s], table[3, s]
        acc1[...] = jnp.zeros((256, 256), F32)
        acc2[...] = jnp.zeros((256, 256), F32)
        acc3[...] = jnp.zeros((16, 256), F32)

        def pair(i, _):
            arrive(table, own, xs, xsem, i)
            pltpu.make_async_copy(h1_in.at[i], h1.at[i], hsem.at[0, i]).wait()
            pltpu.make_async_copy(h2_in.at[i], h2.at[i], hsem.at[1, i]).wait()
            rows = pl.ds(pl.multiple_of(i * 8, 8), 8)
            d_raw = jnp.concatenate([dr[0, rows, :], dr[1, rows, :]], 1)
            d_raw = jnp.concatenate([d_raw, jnp.zeros((8, 256), F32)], 0).astype(BF16)
            x = xs[i].reshape(256, 256)
            one, two = h1[i], h2[i]
            acc3[...] += jnp.dot(d_raw, two, preferred_element_type=F32)
            dh = lax.dot_general(
                d_raw, wv[s, 256:272], (((0,), (0,)), ((), ())), preferred_element_type=F32
            )
            d_two = jnp.where(two > 0, dh, 0.0).astype(BF16)
            acc2[...] += lax.dot_general(
                one, d_two, (((0,), (0,)), ((), ())), preferred_element_type=F32
            )
            dh = lax.dot_general(
                d_two, wv[s, 0:256], (((1,), (1,)), ((), ())), preferred_element_type=F32
            )
            d_one = jnp.where(one > 0, dh, 0.0).astype(BF16)
            acc1[...] += lax.dot_general(
                x, d_one, (((0,), (0,)), ((), ())), preferred_element_type=F32
            )
            return 0

        lax.fori_loop(begin, begin + count, pair, 0)
        stage[s, 0:256] = acc1[...].astype(BF16)
        stage[s, 256:512] = acc2[...].astype(BF16)
        stage[s, 512:528] = acc3[...].astype(BF16)
        pltpu.make_async_copy(stage.at[s], grads[s], gsem.at[s]).start()
    for s in range(NS):
        pltpu.make_async_copy(stage.at[s], grads[s], gsem.at[s]).wait()


def spec(space):
    return pl.BlockSpec(memory_space=space)


def local(
    features, deltas, weight_one, weight_two, weight_out, target, block_region, seg_order, owner_map
):
    smem, vmem, hbm = spec(pltpu.SMEM), spec(pltpu.VMEM), spec(pl.ANY)
    shape = jax.ShapeDtypeStruct
    me = lax.axis_index("region")
    place = jnp.stack([me >> 3, (me >> 1) & 3, me & 1]).astype(I32)

    def swap(a):
        return lax.ppermute(a, "region", move("core", 1))

    head = jnp.pad(weight_out[0].T, ((0, 12), (0, 0)))
    held = {(0, 0): jnp.concatenate([weight_one[0], weight_two[0], head], 0)}
    for key, source, axis, step in TREE:
        held[key] = lax.ppermute(held[source], "region", move(axis, -step))
    weights = [held[(s // 4, s % 4)] for s in range(NS)]

    meta = pl.pallas_call(
        meta_kernel,
        out_shape=shape((8, 128), F32),
        in_specs=[smem, smem, vmem, vmem, vmem],
        out_specs=vmem,
        name="meta",
    )(place, owner_map, block_region, seg_order, target)
    meta_sib = swap(meta)
    x_sib, d_sib = swap(features), swap(deltas)
    table, code = pl.pallas_call(
        plan_kernel,
        out_shape=(shape((8, 128), I32), shape((8, 128), I32)),
        in_specs=[smem, vmem, vmem],
        out_specs=(vmem, vmem),
        name="plan",
    )(place, meta, meta_sib)

    dma = pltpu.SemaphoreType.DMA
    res, saved, h1, h2 = pl.pallas_call(
        forward_kernel,
        out_shape=(
            shape((8, 128), F32),
            shape((6, NP, 256), F32),
            shape((NP, 256, 256), BF16),
            shape((NP, 256, 256), BF16),
        ),
        in_specs=[smem, vmem, hbm, hbm, vmem, vmem] + [hbm] * NS,
        out_specs=(vmem, vmem, hbm, hbm),
        scratch_shapes=[
            pltpu.VMEM((NP, 2, 128, 256), BF16),
            pltpu.VMEM((NS, ROWS, 256), BF16),
            pltpu.VMEM((NP, 256, 256), BF16),
            pltpu.VMEM((NP, 256, 256), BF16),
            pltpu.VMEM((2, NP * 8, 128), F32),
            dma((NP, 2)),
            dma((NS,)),
            dma((2, NP)),
        ],
        compiler_params=VMEM,
        name="forward",
    )(table, code, features, x_sib, deltas, d_sib, *weights)
    res_sib = swap(res)
    color, *grads = pl.pallas_call(
        backward_kernel,
        out_shape=(shape((8, 128), F32),) + (shape((ROWS, 256), BF16),) * NS,
        in_specs=[smem, vmem, hbm, hbm, vmem, vmem, vmem, vmem, vmem, hbm, hbm] + [hbm] * NS,
        out_specs=(vmem,) + (hbm,) * NS,
        scratch_shapes=[
            pltpu.VMEM((NP, 2, 128, 256), BF16),
            pltpu.VMEM((NS, 272, 256), BF16),
            pltpu.VMEM((NP, 256, 256), BF16),
            pltpu.VMEM((NP, 256, 256), BF16),
            pltpu.VMEM((2, NP * 8, 128), F32),
            pltpu.VMEM((256, 256), F32),
            pltpu.VMEM((256, 256), F32),
            pltpu.VMEM((16, 256), F32),
            pltpu.VMEM((NS, ROWS, 256), BF16),
            dma((NP, 2)),
            dma((NS,)),
            dma((2, NP)),
            dma((NS,)),
        ],
        compiler_params=VMEM,
        name="backward",
    )(table, code, features, x_sib, res, res_sib, meta, meta_sib, saved, h1, h2, *weights)

    sums = {(s // 4, s % 4): grads[s] for s in range(NS)}
    for key, source, axis, step in reversed(TREE):
        got = lax.ppermute(sums[key], "region", move(axis, step))
        sums[source] = (sums[source].astype(F32) + got.astype(F32)).astype(BF16)
    mine = sums[(0, 0)]
    total = mine.astype(F32)
    for d in (1, 3, 2):
        got = lax.ppermute(mine, "ray", [(i, (i + d) % 4) for i in range(4)])
        total = total + got.astype(F32)
    ray_color = color[0:3, 0:64:4].T
    return ray_color, total[None, 0:256], total[None, 256:512], total[512:516].T[None]


def solution(mesh):
    in_specs = (
        P(("ray", "region"), None, None),
        P(("ray", "region"), None),
        P("region", None, None),
        P("region", None, None),
        P("region", None, None),
        P(("ray", "region"), None),
        P(("ray", "region"), None),
        P(("ray", "region"), None),
        P(),
    )
    out_specs = (
        P(("ray", "region"), None),
        P("region", None, None),
        P("region", None, None),
        P("region", None, None),
    )
    return jax.shard_map(local, mesh=mesh, in_specs=in_specs, out_specs=out_specs, check_vma=False)
```

```python
import functools

import jax
import jax.numpy as jnp
from jax import lax
from jax.experimental import pallas as pl
from jax.experimental.pallas import tpu as pltpu
from jax.sharding import PartitionSpec as P

F32, BF16, I32 = jnp.float32, jnp.bfloat16, jnp.int32
G = 4
NS = 16
NP = 64
ROWS = 528
MIB = 1024 * 1024
HI = lax.Precision.HIGHEST

TREE = (
    ((0, 1), (0, 0), "x", 1),
    ((0, 3), (0, 0), "x", 3),
    ((1, 0), (0, 0), "z", 1),
    ((3, 0), (0, 0), "z", 3),
    ((0, 2), (0, 1), "x", 1),
    ((1, 3), (1, 0), "x", 3),
    ((2, 0), (1, 0), "z", 1),
    ((3, 3), (0, 3), "z", 3),
    ((1, 1), (1, 0), "x", 1),
    ((3, 1), (0, 1), "z", 3),
    ((1, 2), (0, 2), "z", 1),
    ((3, 2), (3, 3), "x", 3),
    ((2, 1), (2, 0), "x", 1),
    ((2, 3), (2, 0), "x", 3),
    ((2, 2), (1, 2), "z", 1),
)


def move(axis, step):
    pairs = []
    for z in range(4):
        for x in range(4):
            for c in range(2):
                z2, x2, c2 = z, x, c
                if axis == "z":
                    z2 = (z + step) % 4
                elif axis == "x":
                    x2 = (x + step) % 4
                else:
                    c2 = 1 - c
                pairs.append((z * 8 + x * 2 + c, z2 * 8 + x2 * 2 + c2))
    return pairs


def iota(shape, dim):
    return lax.broadcasted_iota(I32, shape, dim)


def meta_kernel(owner, region, order, target, delta, out):
    me = lax.axis_index("region")
    spot = region[...]
    slot = jnp.zeros((1, 64), I32)
    for r in range(32):
        slot = jnp.where(spot == r, owner[r], slot)
    dz = ((slot >> 3) - (me >> 3)) & 3
    dx = (((slot >> 1) & 3) - ((me >> 1) & 3)) & 3
    key = (dz * 4 + dx) * 2 + (slot & 1)
    rows = jnp.concatenate([order[...].astype(F32), target[...], jnp.zeros((1, 16), F32)], 0)
    ray = jnp.where((iota((16, 64), 1) >> 2) == iota((16, 64), 0), 1.0, 0.0)
    spread = jnp.dot(rows, ray, precision=HI, preferred_element_type=F32)
    pick = (iota((8, 64), 1) & 3) == iota((8, 64), 0)
    place = jnp.sum(jnp.where(pick, spread, 0.0), 0, keepdims=True)
    top = jnp.concatenate([key.astype(F32), place, spread[4:7], jnp.zeros((3, 64), F32)], 0)
    out[0:8, :] = jnp.concatenate([top, jnp.zeros((8, 64), F32)], 1)
    out[8:72, :] = delta[...].astype(F32)


def both(a, b):
    lane = iota(a.shape, 1)
    return jnp.where(lane < 64, a, pltpu.roll(b, 64, 1))


def plan_kernel(own, sib, table, code_out):
    meta = both(own[0:8], sib[0:8])
    key = meta[0:1].astype(I32)
    rel, valid = key >> 1, (key & 1) == (lax.axis_index("region") & 1)
    hot = (iota((NS, 128), 0) == rel) & valid
    hotf = jnp.where(hot, 1.0, 0.0)
    before = jnp.where(iota((128, 128), 0) < iota((128, 128), 1), 1.0, 0.0)
    cum = jnp.dot(hotf, before, preferred_element_type=F32)
    rank = jnp.sum(hotf * cum, 0, keepdims=True).astype(I32)
    count = jnp.sum(hotf, 1, keepdims=True).astype(I32)
    pairs = ((count + 1) >> 1).astype(F32)
    eye = iota((NS, 128), 0) == iota((NS, 128), 1)
    pairs_row = jnp.sum(jnp.where(eye, pairs, 0.0), 0, keepdims=True)
    ahead = iota((NS, 128), 1) < iota((NS, 128), 0)
    start = jnp.sum(jnp.where(ahead, pairs_row, 0.0), 1, keepdims=True)
    start_row = jnp.sum(jnp.where(eye, start, 0.0), 0, keepdims=True)
    start_j = jnp.sum(hotf * start, 0, keepdims=True).astype(I32)
    code = start_j + (rank >> 1) + (rank & 1) * NP
    code = jnp.where(valid, code, -1)
    square = iota((128, 128), 0) == iota((128, 128), 1)
    code_col = jnp.sum(jnp.where(square, code.astype(F32), 0.0), 1, keepdims=True)
    source = (iota((128, 128), 0) + 1).astype(F32)
    hit = code_col.astype(I32) == iota((128, 128), 1)
    inverse = jnp.sum(jnp.where(hit, source, 0.0), 0, keepdims=True).astype(I32)
    inverse = jnp.maximum(inverse - 1, 0)
    begun = jnp.where(start.astype(I32) <= iota((NS, 128), 1), 1.0, 0.0)
    slot_of = jnp.sum(begun, 0, keepdims=True).astype(I32) - 1
    total = jnp.sum(pairs_row, 1, keepdims=True).astype(I32)
    table[...] = jnp.concatenate(
        [
            inverse,
            slot_of,
            start_row.astype(I32),
            pairs_row.astype(I32),
            jnp.broadcast_to(total, (1, 128)),
            jnp.zeros((3, 128), I32),
        ],
        0,
    )
    code_out[...] = jnp.broadcast_to(code, (8, 128))


def fetch(table, own, sib, xs, sems, groups):
    def step(t, _):
        for g in range(G):
            for h in range(2):
                i = t * G + g
                src = table[0, h * NP + i]
                dst = xs.at[i, pl.ds(128 * h, 128)]

                @pl.when(src < 64)
                def _():
                    pltpu.make_async_copy(own.at[src], dst, sems.at[t]).start()

                @pl.when(src >= 64)
                def _():
                    pltpu.make_async_copy(sib.at[src - 64], dst, sems.at[t]).start()

        return 0

    lax.fori_loop(0, groups, step, 0)


def forward_kernel(*refs):
    table, code, own, sib, m_own, m_sib = refs[:6]
    weights = refs[6 : 6 + NS]
    res, saved, xs, wv, h1, h2 = refs[6 + NS : 12 + NS]
    raw, xsem, wsem = refs[12 + NS :]
    groups = (table[4, 0] + G - 1) // G
    for s in range(NS):
        pltpu.make_async_copy(weights[s], wv.at[s], wsem).start()
    fetch(table, own, sib, xs, xsem, groups)
    raw[...] = jnp.zeros(raw.shape, F32)
    pltpu.make_async_copy(wv, wv, wsem).wait()

    def step(t, _):
        ids = [G * t + g for g in range(G)]
        slots = [table[1, i] for i in ids]
        chunk = xs.at[pl.ds(G * t, G)]
        pltpu.make_async_copy(chunk, chunk, xsem.at[t]).wait()
        pre = [
            jnp.dot(xs[i], wv[s, 0:256], preferred_element_type=F32)
            for i, s in zip(ids, slots)
        ]
        one = [jnp.maximum(p, 0.0).astype(BF16) for p in pre]
        pre = [
            jnp.dot(o, wv[s, 256:512], preferred_element_type=F32) for o, s in zip(one, slots)
        ]
        two = [jnp.maximum(p, 0.0).astype(BF16) for p in pre]
        out = [
            lax.dot_general(
                wv[s, 512:528], o, (((1,), (1,)), ((), ())), preferred_element_type=F32
            )
            for o, s in zip(two, slots)
        ]
        for g, i in enumerate(ids):
            h1[i] = one[g]
            h2[i] = two[g]
            rows = pl.ds(pl.multiple_of(i * 8, 8), 8)
            raw[0, rows, :] = out[g][0:8, 0:128]
            raw[1, rows, :] = out[g][0:8, 128:256]
        return 0

    lax.fori_loop(0, groups, step, 0)

    before = jnp.where(iota((128, 128), 0) < iota((128, 128), 1), 1.0, 0.0)
    spot = code[0:1]
    out = jnp.zeros((4, 128), F32)
    for h in range(2):
        lanes = slice(h * 128, h * 128 + 128)
        pick = spot == iota((NP, 128), 0) + h * NP
        pickb = jnp.where(pick, 1.0, 0.0).astype(BF16)
        deltas = jnp.concatenate([m_own[8:72], m_sib[8:72]], 0).astype(BF16)
        delta = jnp.dot(pickb, deltas, preferred_element_type=F32)
        ch = [raw[h, pl.ds(c, NP, stride=8), :] for c in range(4)]
        sigma = jnp.maximum(ch[0], 0.0) + jnp.log1p(jnp.exp(-jnp.abs(ch[0])))
        rgb = [jax.nn.sigmoid(ch[c]) for c in (1, 2, 3)]
        tau = sigma * delta
        cum = jnp.dot(tau, before, precision=HI, preferred_element_type=F32)
        trans = jnp.exp(-cum)
        opacity = 1.0 - jnp.exp(-tau)
        weight = trans * opacity
        cols = [jnp.sum(weight * rgb[c], 1, keepdims=True) for c in range(3)]
        cols.append(-jnp.sum(tau, 1, keepdims=True))
        out += jnp.concatenate(
            [jnp.sum(jnp.where(pick, col, 0.0), 0, keepdims=True) for col in cols], 0
        )
        keep = rgb + [weight, trans * (1.0 - opacity), delta * jax.nn.sigmoid(ch[0])]
        for k in range(6):
            saved[k, :, lanes] = keep[k]
    res[...] = jnp.concatenate([out, jnp.zeros((4, 128), F32)], 0)


def backward_kernel(*refs):
    table, code, res, res_sib, m_own, m_sib, saved, xs, wv, h1, h2, color_out = refs[:12]
    grads = refs[12 : 12 + NS]
    dr, acc1, acc2, acc3, stage, gsem = refs[12 + NS :]
    groups = (table[4, 0] + G - 1) // G

    meta = both(m_own[0:8], m_sib[0:8])
    parts = res[...] + pltpu.roll(res_sib[...], 64, 1)
    order = meta[1:2]
    square = (128, 128)
    same = (iota(square, 0) >> 2) == (iota(square, 1) >> 2)
    samef = jnp.where(same, 1.0, 0.0)
    eye = iota(square, 0) == iota(square, 1)
    order_col = jnp.sum(jnp.where(eye, order, 0.0), 1, keepdims=True)
    prior = jnp.where(same & (order_col < order), 1.0, 0.0)
    later = jnp.where(same & (order_col > order), 1.0, 0.0)
    ahead = jnp.dot(parts, prior, precision=HI, preferred_element_type=F32)[3:4]
    reach = jnp.exp(ahead)
    shown = parts * reach
    color = jnp.dot(shown, samef, precision=HI, preferred_element_type=F32)
    color_out[...] = color
    gray = color[0:3] - meta[2:5]
    portion = jnp.sum(shown[0:3] * gray, 0, keepdims=True)
    log_cot = jnp.dot(
        jnp.broadcast_to(portion, (8, 128)), later, precision=HI, preferred_element_type=F32
    )[0:1]
    cot = [reach * gray[c : c + 1] for c in range(3)] + [log_cot]

    after = jnp.where(iota(square, 0) > iota(square, 1), 1.0, 0.0)
    spot = code[0:1]
    dr[...] = jnp.zeros(dr.shape, F32)
    for h in range(2):
        lanes = slice(h * 128, h * 128 + 128)
        pick = spot == iota((NP, 128), 0) + h * NP
        col = [jnp.sum(jnp.where(pick, row, 0.0), 1, keepdims=True) for row in cot]
        rgb = [saved[c, :, lanes] for c in range(3)]
        weight = saved[3, :, lanes]
        d_weight = rgb[0] * col[0] + rgb[1] * col[1] + rgb[2] * col[2]
        follow = jnp.dot(d_weight * weight, after, precision=HI, preferred_element_type=F32)
        d_tau = d_weight * saved[4, :, lanes] - col[3] - follow
        dr[h, pl.ds(0, NP, stride=8), :] = d_tau * saved[5, :, lanes]
        for c in range(3):
            d_col = weight * col[c] * rgb[c] * (1.0 - rgb[c])
            dr[h, pl.ds(c + 1, NP, stride=8), :] = d_col

    def send(s):
        pltpu.make_async_copy(stage.at[s], grads[s], gsem).start()

    for s in range(NS):

        @pl.when(table[3, s] == 0)
        def _():
            stage[s] = jnp.zeros((ROWS, 256), BF16)
            send(s)

    def step(t, _):
        ids = [G * t + g for g in range(G)]
        slots = [table[1, i] for i in ids]
        tn, nt = (((0,), (0,)), ((), ())), (((1,), (1,)), ((), ()))
        raws = []
        for i in ids:
            rows = pl.ds(pl.multiple_of(i * 8, 8), 8)
            d_raw = jnp.concatenate([dr[0, rows, :], dr[1, rows, :]], 1)
            raws.append(jnp.concatenate([d_raw, jnp.zeros((8, 256), F32)], 0).astype(BF16))
        two = [h2[i] for i in ids]
        dh = [
            lax.dot_general(r, wv[s, 512:528], tn, preferred_element_type=F32)
            for r, s in zip(raws, slots)
        ]
        d_two = [jnp.where(h > 0, d, 0.0).astype(BF16) for h, d in zip(two, dh)]
        one = [h1[i] for i in ids]
        dh = [
            lax.dot_general(d, wv[s, 256:512], nt, preferred_element_type=F32)
            for d, s in zip(d_two, slots)
        ]
        g3 = [jnp.dot(r, h, preferred_element_type=F32) for r, h in zip(raws, two)]
        g2 = [
            lax.dot_general(h, d, tn, preferred_element_type=F32) for h, d in zip(one, d_two)
        ]
        d_one = [jnp.where(h > 0, d, 0.0).astype(BF16) for h, d in zip(one, dh)]
        g1 = [
            lax.dot_general(xs[i], d, tn, preferred_element_type=F32)
            for i, d in zip(ids, d_one)
        ]
        for g, s in enumerate(slots):
            first = ids[g] == table[2, s]
            acc1[s] = jnp.where(first, 0.0, acc1[s]) + g1[g]
            acc2[s] = jnp.where(first, 0.0, acc2[s]) + g2[g]
            acc3[s] = jnp.where(first, 0.0, acc3[s]) + g3[g]
        return 0

    lax.fori_loop(0, groups, step, 0)
    for s in range(NS):

        @pl.when(table[3, s] > 0)
        def _():
            stage[s, 0:256] = acc1[s].astype(BF16)
            stage[s, 256:512] = acc2[s].astype(BF16)
            stage[s, 512:528] = acc3[s].astype(BF16)
            send(s)

    pltpu.make_async_copy(stage, stage, gsem).wait()


def spec(space):
    return pl.BlockSpec(memory_space=space)


def local(
    features, deltas, weight_one, weight_two, weight_out, target, block_region, seg_order, owner_map
):
    smem, vmem, hbm = spec(pltpu.SMEM), spec(pltpu.VMEM), spec(pl.ANY)
    shape = jax.ShapeDtypeStruct
    def swap(a):
        return lax.ppermute(a, "region", move("core", 1))

    head = jnp.pad(weight_out[0].T, ((0, 12), (0, 0)))
    held = {(0, 0): jnp.concatenate([weight_one[0], weight_two[0], head], 0)}
    for key, source, axis, step in TREE:
        held[key] = lax.ppermute(held[source], "region", move(axis, -step))
    weights = [held[(s // 4, s % 4)] for s in range(NS)]

    meta = pl.pallas_call(
        meta_kernel,
        out_shape=shape((72, 128), F32),
        in_specs=[smem, vmem, vmem, vmem, vmem],
        out_specs=vmem,
        name="meta",
    )(owner_map, block_region.T, seg_order.T, target.T, deltas)
    meta_sib, x_sib = swap(meta), swap(features)
    table, code = pl.pallas_call(
        plan_kernel,
        out_shape=(shape((8, 128), I32), shape((8, 128), I32)),
        in_specs=[vmem, vmem],
        out_specs=(vmem, vmem),
        name="plan",
    )(meta, meta_sib)

    dma = pltpu.SemaphoreType.DMA
    kept = pltpu.VMEM((NP, 256, 256), BF16)
    res, saved, xs, wv, h1, h2 = pl.pallas_call(
        forward_kernel,
        out_shape=(
            shape((8, 128), F32),
            pltpu.VMEM((6, NP, 256), F32),
            kept,
            pltpu.VMEM((NS, ROWS, 256), BF16),
            kept,
            kept,
        ),
        in_specs=[smem, vmem, hbm, hbm, vmem, vmem] + [hbm] * NS,
        out_specs=(vmem,) * 6,
        scratch_shapes=[pltpu.VMEM((2, NP * 8, 128), F32), dma((NP // G,)), dma],
        compiler_params=pltpu.CompilerParams(vmem_limit_bytes=8 * MIB),
        name="forward",
    )(table, code, features, x_sib, meta, meta_sib, *weights)
    res_sib = swap(res)
    color, *grads = pl.pallas_call(
        backward_kernel,
        out_shape=(shape((8, 128), F32),) + (shape((ROWS, 256), BF16),) * NS,
        in_specs=[smem] + [vmem] * 10,
        out_specs=(vmem,) + (hbm,) * NS,
        scratch_shapes=[
            pltpu.VMEM((2, NP * 8, 128), F32),
            pltpu.VMEM((NS, 256, 256), F32),
            pltpu.VMEM((NS, 256, 256), F32),
            pltpu.VMEM((NS, 16, 256), F32),
            pltpu.VMEM((NS, ROWS, 256), BF16),
            dma,
        ],
        compiler_params=pltpu.CompilerParams(vmem_limit_bytes=18 * MIB),
        name="backward",
    )(table, code, res, res_sib, meta, meta_sib, saved, xs, wv, h1, h2)

    sums = {(s // 4, s % 4): grads[s] for s in range(NS)}
    for key, source, axis, step in reversed(TREE):
        got = lax.ppermute(sums[key], "region", move(axis, step))
        sums[source] = (sums[source].astype(F32) + got.astype(F32)).astype(BF16)
    mine = sums[(0, 0)]
    total = mine.astype(F32)
    for d in (1, 3, 2):
        got = lax.ppermute(mine, "ray", [(i, (i + d) % 4) for i in range(4)])
        total = total + got.astype(F32)
    ray_color = color[0:3, 0:64:4].T
    return ray_color, total[None, 0:256], total[None, 256:512], total[512:516].T[None]


def solution(mesh):
    in_specs = (
        P(("ray", "region"), None, None),
        P(("ray", "region"), None),
        P("region", None, None),
        P("region", None, None),
        P("region", None, None),
        P(("ray", "region"), None),
        P(("ray", "region"), None),
        P(("ray", "region"), None),
        P(),
    )
    out_specs = (
        P(("ray", "region"), None),
        P("region", None, None),
        P("region", None, None),
        P("region", None, None),
    )
    return jax.shard_map(local, mesh=mesh, in_specs=in_specs, out_specs=out_specs, check_vma=False)
```

```python
import functools

import jax
import jax.numpy as jnp
from jax import lax
from jax.experimental import pallas as pl
from jax.experimental.pallas import tpu as pltpu
from jax.sharding import PartitionSpec as P

F32, BF16, I32 = jnp.float32, jnp.bfloat16, jnp.int32
G = 4
NS = 16
NP = 64
ROWS = 528
MIB = 1024 * 1024
HI = lax.Precision.HIGHEST

TREE = (
    ((0, 1), (0, 0), "x", 1),
    ((0, 3), (0, 0), "x", 3),
    ((1, 0), (0, 0), "z", 1),
    ((3, 0), (0, 0), "z", 3),
    ((0, 2), (0, 1), "x", 1),
    ((1, 3), (1, 0), "x", 3),
    ((2, 0), (1, 0), "z", 1),
    ((3, 3), (0, 3), "z", 3),
    ((1, 1), (1, 0), "x", 1),
    ((3, 1), (0, 1), "z", 3),
    ((1, 2), (0, 2), "z", 1),
    ((3, 2), (3, 3), "x", 3),
    ((2, 1), (2, 0), "x", 1),
    ((2, 3), (2, 0), "x", 3),
    ((2, 2), (1, 2), "z", 1),
)


def move(axis, step):
    pairs = []
    for z in range(4):
        for x in range(4):
            for c in range(2):
                z2, x2, c2 = z, x, c
                if axis == "z":
                    z2 = (z + step) % 4
                elif axis == "x":
                    x2 = (x + step) % 4
                else:
                    c2 = 1 - c
                pairs.append((z * 8 + x * 2 + c, z2 * 8 + x2 * 2 + c2))
    return pairs


def iota(shape, dim):
    return lax.broadcasted_iota(I32, shape, dim)


def meta_kernel(owner, region, order, target, delta, out):
    me = lax.axis_index("region")
    spot = region[...]
    slot = jnp.zeros((1, 64), I32)
    for r in range(32):
        slot = jnp.where(spot == r, owner[r], slot)
    dz = ((slot >> 3) - (me >> 3)) & 3
    dx = (((slot >> 1) & 3) - ((me >> 1) & 3)) & 3
    key = (dz * 4 + dx) * 2 + (slot & 1)
    rows = jnp.concatenate([order[...].astype(F32), target[...], jnp.zeros((1, 16), F32)], 0)
    ray = jnp.where((iota((16, 64), 1) >> 2) == iota((16, 64), 0), 1.0, 0.0)
    spread = jnp.dot(rows, ray, precision=HI, preferred_element_type=F32)
    pick = (iota((8, 64), 1) & 3) == iota((8, 64), 0)
    place = jnp.sum(jnp.where(pick, spread, 0.0), 0, keepdims=True)
    top = jnp.concatenate([key.astype(F32), place, spread[4:7], jnp.zeros((3, 64), F32)], 0)
    out[0:8, :] = jnp.concatenate([top, jnp.zeros((8, 64), F32)], 1)
    out[8:72, :] = delta[...].astype(F32)


def both(a, b):
    lane = iota(a.shape, 1)
    return jnp.where(lane < 64, a, pltpu.roll(b, 64, 1))


def plan_kernel(own, sib, x_own, x_sib, table, info, xa, sems):
    copies = []
    for k in range(8):
        src = (x_own, x_sib)[k // 4].at[pl.ds(k % 4 * 16, 16)]
        copies.append(pltpu.make_async_copy(src, xa.at[pl.ds(k * 16, 16)], sems.at[k]))
        copies[k].start()
    meta = both(own[0:8], sib[0:8])
    key = meta[0:1].astype(I32)
    rel, valid = key >> 1, (key & 1) == (lax.axis_index("region") & 1)
    hot = (iota((NS, 128), 0) == rel) & valid
    hotf = jnp.where(hot, 1.0, 0.0)
    before = jnp.where(iota((128, 128), 0) < iota((128, 128), 1), 1.0, 0.0)
    cum = jnp.dot(hotf, before, preferred_element_type=F32)
    rank = jnp.sum(hotf * cum, 0, keepdims=True).astype(I32)
    count = jnp.sum(hotf, 1, keepdims=True).astype(I32)
    pairs = ((count + 1) >> 1).astype(F32)
    eye = iota((NS, 128), 0) == iota((NS, 128), 1)
    pairs_row = jnp.sum(jnp.where(eye, pairs, 0.0), 0, keepdims=True)
    ahead = iota((NS, 128), 1) < iota((NS, 128), 0)
    start = jnp.sum(jnp.where(ahead, pairs_row, 0.0), 1, keepdims=True)
    start_row = jnp.sum(jnp.where(eye, start, 0.0), 0, keepdims=True)
    start_j = jnp.sum(hotf * start, 0, keepdims=True).astype(I32)
    code = start_j + (rank >> 1) + (rank & 1) * NP
    code = jnp.where(valid, code, -1)
    square = iota((128, 128), 0) == iota((128, 128), 1)
    code_col = jnp.sum(jnp.where(square, code.astype(F32), 0.0), 1, keepdims=True)
    source = (iota((128, 128), 0) + 1).astype(F32)
    hit = code_col.astype(I32) == iota((128, 128), 1)
    inverse = jnp.sum(jnp.where(hit, source, 0.0), 0, keepdims=True).astype(I32)
    inverse = jnp.maximum(inverse - 1, 0)
    begun = jnp.where(start.astype(I32) <= iota((NS, 128), 1), 1.0, 0.0)
    slot_of = jnp.sum(begun, 0, keepdims=True).astype(I32) - 1
    total = jnp.sum(pairs_row, 1, keepdims=True).astype(I32)
    table[...] = jnp.concatenate(
        [
            inverse,
            slot_of,
            start_row.astype(I32),
            pairs_row.astype(I32),
            jnp.broadcast_to(total, (1, 128)),
            jnp.zeros((3, 128), I32),
        ],
        0,
    )
    info[0:8, :] = meta
    info[8:16, :] = jnp.broadcast_to(code, (8, 128)).astype(F32)
    info[16:80, :] = own[8:72]
    info[80:144, :] = sib[8:72]
    for copy in copies:
        copy.wait()


def samples(table, xa, i):
    return jnp.concatenate([xa[table[0, i]], xa[table[0, NP + i]]], 0)


def forward_kernel(*refs):
    table, info, xa = refs[:3]
    weights = refs[3 : 3 + NS]
    res, saved, wv, h1, h2 = refs[3 + NS : 8 + NS]
    raw, wsem = refs[8 + NS :]
    groups = (table[4, 0] + G - 1) // G
    for s in range(NS):
        pltpu.make_async_copy(weights[s], wv.at[s], wsem.at[s]).start()
    raw[...] = jnp.zeros(raw.shape, F32)

    def held(s, _):
        pltpu.make_async_copy(weights[0], wv.at[s], wsem.at[s]).wait()
        return 0

    def step(t, ready):
        ids = [G * t + g for g in range(G)]
        slots = [table[1, i] for i in ids]
        lax.fori_loop(ready, slots[-1] + 1, held, 0)
        pre = [
            jnp.dot(samples(table, xa, i), wv[s, 0:256], preferred_element_type=F32)
            for i, s in zip(ids, slots)
        ]
        one = [jnp.maximum(p, 0.0).astype(BF16) for p in pre]
        pre = [
            jnp.dot(o, wv[s, 256:512], preferred_element_type=F32) for o, s in zip(one, slots)
        ]
        two = [jnp.maximum(p, 0.0).astype(BF16) for p in pre]
        out = [
            lax.dot_general(
                wv[s, 512:528], o, (((1,), (1,)), ((), ())), preferred_element_type=F32
            )
            for o, s in zip(two, slots)
        ]
        for g, i in enumerate(ids):
            h1[i] = one[g]
            h2[i] = two[g]
            rows = pl.ds(pl.multiple_of(i * 8, 8), 8)
            raw[0, rows, :] = out[g][0:8, 0:128]
            raw[1, rows, :] = out[g][0:8, 128:256]
        return slots[-1] + 1

    lax.fori_loop(lax.fori_loop(0, groups, step, 0), NS, held, 0)

    before = jnp.where(iota((128, 128), 0) < iota((128, 128), 1), 1.0, 0.0)
    spot = info[8:9].astype(I32)
    out = jnp.zeros((4, 128), F32)
    for h in range(2):
        lanes = slice(h * 128, h * 128 + 128)
        pick = spot == iota((NP, 128), 0) + h * NP
        pickb = jnp.where(pick, 1.0, 0.0).astype(BF16)
        deltas = info[16:144].astype(BF16)
        delta = jnp.dot(pickb, deltas, preferred_element_type=F32)
        ch = [raw[h, pl.ds(c, NP, stride=8), :] for c in range(4)]
        sigma = jnp.maximum(ch[0], 0.0) + jnp.log1p(jnp.exp(-jnp.abs(ch[0])))
        rgb = [jax.nn.sigmoid(ch[c]) for c in (1, 2, 3)]
        tau = sigma * delta
        cum = jnp.dot(tau, before, precision=HI, preferred_element_type=F32)
        trans = jnp.exp(-cum)
        opacity = 1.0 - jnp.exp(-tau)
        weight = trans * opacity
        cols = [jnp.sum(weight * rgb[c], 1, keepdims=True) for c in range(3)]
        cols.append(-jnp.sum(tau, 1, keepdims=True))
        out += jnp.concatenate(
            [jnp.sum(jnp.where(pick, col, 0.0), 0, keepdims=True) for col in cols], 0
        )
        keep = rgb + [weight, trans * (1.0 - opacity), delta * jax.nn.sigmoid(ch[0])]
        for k in range(6):
            saved[k, :, lanes] = keep[k]
    res[...] = jnp.concatenate([out, jnp.zeros((4, 128), F32)], 0)


def backward_kernel(*refs):
    table, info, res, res_sib, xa, saved, wv, h1, h2, color_out = refs[:10]
    grads = refs[10 : 10 + NS]
    dr, acc1, acc2, acc3 = refs[10 + NS :]
    groups = (table[4, 0] + G - 1) // G

    meta = info[0:8]
    parts = res[...] + pltpu.roll(res_sib[...], 64, 1)
    order = meta[1:2]
    square = (128, 128)
    same = (iota(square, 0) >> 2) == (iota(square, 1) >> 2)
    samef = jnp.where(same, 1.0, 0.0)
    eye = iota(square, 0) == iota(square, 1)
    order_col = jnp.sum(jnp.where(eye, order, 0.0), 1, keepdims=True)
    prior = jnp.where(same & (order_col < order), 1.0, 0.0)
    later = jnp.where(same & (order_col > order), 1.0, 0.0)
    ahead = jnp.dot(parts, prior, precision=HI, preferred_element_type=F32)[3:4]
    reach = jnp.exp(ahead)
    shown = parts * reach
    color = jnp.dot(shown, samef, precision=HI, preferred_element_type=F32)
    color_out[...] = color
    gray = color[0:3] - meta[2:5]
    portion = jnp.sum(shown[0:3] * gray, 0, keepdims=True)
    log_cot = jnp.dot(
        jnp.broadcast_to(portion, (8, 128)), later, precision=HI, preferred_element_type=F32
    )[0:1]
    cot = [reach * gray[c : c + 1] for c in range(3)] + [log_cot]

    after = jnp.where(iota(square, 0) > iota(square, 1), 1.0, 0.0)
    spot = info[8:9].astype(I32)
    dr[...] = jnp.zeros(dr.shape, F32)
    for h in range(2):
        lanes = slice(h * 128, h * 128 + 128)
        pick = spot == iota((NP, 128), 0) + h * NP
        col = [jnp.sum(jnp.where(pick, row, 0.0), 1, keepdims=True) for row in cot]
        rgb = [saved[c, :, lanes] for c in range(3)]
        weight = saved[3, :, lanes]
        d_weight = rgb[0] * col[0] + rgb[1] * col[1] + rgb[2] * col[2]
        follow = jnp.dot(d_weight * weight, after, precision=HI, preferred_element_type=F32)
        d_tau = d_weight * saved[4, :, lanes] - col[3] - follow
        dr[h, pl.ds(0, NP, stride=8), :] = d_tau * saved[5, :, lanes]
        for c in range(3):
            d_col = weight * col[c] * rgb[c] * (1.0 - rgb[c])
            dr[h, pl.ds(c + 1, NP, stride=8), :] = d_col

    for s in range(NS):

        @pl.when(table[3, s] == 0)
        def _():
            grads[s][...] = jnp.zeros((ROWS, 256), BF16)

    def step(t, _):
        ids = [G * t + g for g in range(G)]
        slots = [table[1, i] for i in ids]
        tn, nt = (((0,), (0,)), ((), ())), (((1,), (1,)), ((), ()))
        raws = []
        for i in ids:
            rows = pl.ds(pl.multiple_of(i * 8, 8), 8)
            d_raw = jnp.concatenate([dr[0, rows, :], dr[1, rows, :]], 1)
            raws.append(jnp.concatenate([d_raw, jnp.zeros((8, 256), F32)], 0).astype(BF16))
        two = [h2[i] for i in ids]
        dh = [
            lax.dot_general(r, wv[s, 512:528], tn, preferred_element_type=F32)
            for r, s in zip(raws, slots)
        ]
        d_two = [jnp.where(h > 0, d, 0.0).astype(BF16) for h, d in zip(two, dh)]
        one = [h1[i] for i in ids]
        dh = [
            lax.dot_general(d, wv[s, 256:512], nt, preferred_element_type=F32)
            for d, s in zip(d_two, slots)
        ]
        g3 = [jnp.dot(r, h, preferred_element_type=F32) for r, h in zip(raws, two)]
        g2 = [
            lax.dot_general(h, d, tn, preferred_element_type=F32) for h, d in zip(one, d_two)
        ]
        d_one = [jnp.where(h > 0, d, 0.0).astype(BF16) for h, d in zip(one, dh)]
        g1 = [
            lax.dot_general(samples(table, xa, i), d, tn, preferred_element_type=F32)
            for i, d in zip(ids, d_one)
        ]
        for g, s in enumerate(slots):
            first = ids[g] == table[2, s]
            acc1[s] = jnp.where(first, 0.0, acc1[s]) + g1[g]
            acc2[s] = jnp.where(first, 0.0, acc2[s]) + g2[g]
            acc3[s] = jnp.where(first, 0.0, acc3[s]) + g3[g]
        return 0

    lax.fori_loop(0, groups, step, 0)
    for s in range(NS):

        @pl.when(table[3, s] > 0)
        def _():
            grads[s][0:256] = acc1[s].astype(BF16)
            grads[s][256:512] = acc2[s].astype(BF16)
            grads[s][512:528] = acc3[s].astype(BF16)


def spec(space):
    return pl.BlockSpec(memory_space=space)


def local(
    features, deltas, weight_one, weight_two, weight_out, target, block_region, seg_order, owner_map
):
    smem, vmem, hbm = spec(pltpu.SMEM), spec(pltpu.VMEM), spec(pl.ANY)
    far = spec(pltpu.MemorySpace.HBM)
    shape = jax.ShapeDtypeStruct
    dma = pltpu.SemaphoreType.DMA
    limit = pltpu.CompilerParams(vmem_limit_bytes=15 * MIB)

    def away(a):
        return pltpu.with_memory_space_constraint(a, pltpu.MemorySpace.HBM)

    def swap(a):
        return lax.ppermute(a, "region", move("core", 1))

    head = jnp.pad(weight_out[0].T, ((0, 12), (0, 0)))
    held = {(0, 0): jnp.concatenate([weight_one[0], weight_two[0], head], 0)}
    x_sib = swap(features)
    for key, source, axis, step in TREE[:4]:
        held[key] = lax.ppermute(held[source], "region", move(axis, -step))
    x_sib, held[(1, 0)] = lax.optimization_barrier((x_sib, held[(1, 0)]))
    for key, source, axis, step in TREE[4:]:
        held[key] = lax.ppermute(held[source], "region", move(axis, -step))
    weights = [held[(s // 4, s % 4)] for s in range(NS)]

    meta = pl.pallas_call(
        meta_kernel,
        out_shape=shape((72, 128), F32),
        in_specs=[smem, vmem, vmem, vmem, vmem],
        out_specs=vmem,
        name="meta",
    )(owner_map, block_region.T, seg_order.T, target.T, deltas)
    meta_sib = swap(meta)
    table, info, xa = pl.pallas_call(
        plan_kernel,
        out_shape=(shape((8, 128), I32), pltpu.VMEM((144, 128), F32), pltpu.VMEM((128, 128, 256), BF16)),
        in_specs=[vmem, vmem, far, hbm],
        out_specs=(vmem,) * 3,
        scratch_shapes=[dma((8,))],
        compiler_params=limit,
        name="plan",
    )(meta, meta_sib, away(features), x_sib)

    kept = pltpu.VMEM((NP, 256, 256), BF16)
    res, saved, wv, h1, h2 = pl.pallas_call(
        forward_kernel,
        out_shape=(
            shape((8, 128), F32),
            pltpu.VMEM((6, NP, 256), F32),
            pltpu.VMEM((NS, ROWS, 256), BF16),
            kept,
            kept,
        ),
        in_specs=[smem, vmem, vmem] + [hbm] * NS,
        out_specs=(vmem,) * 5,
        scratch_shapes=[pltpu.VMEM((2, NP * 8, 128), F32), dma((NS,))],
        compiler_params=limit,
        name="forward",
    )(table, info, xa, *weights)
    res_sib = swap(res)
    color, *grads = pl.pallas_call(
        backward_kernel,
        out_shape=(shape((8, 128), F32),) + (pltpu.VMEM((ROWS, 256), BF16),) * NS,
        in_specs=[smem] + [vmem] * 8,
        out_specs=(vmem,) * (NS + 1),
        scratch_shapes=[
            pltpu.VMEM((2, NP * 8, 128), F32),
            pltpu.VMEM((NS, 256, 256), F32),
            pltpu.VMEM((NS, 256, 256), F32),
            pltpu.VMEM((NS, 16, 256), F32),
        ],
        compiler_params=limit,
        name="backward",
    )(table, info, res, res_sib, xa, saved, wv, h1, h2)

    sums = {(s // 4, s % 4): grads[s] for s in range(NS)}
    for key, source, axis, step in reversed(TREE):
        got = lax.ppermute(sums[key], "region", move(axis, step))
        sums[source] = (sums[source].astype(F32) + got.astype(F32)).astype(BF16)
    mine = sums[(0, 0)]
    total = mine.astype(F32)
    for d in (1, 3, 2):
        got = lax.ppermute(mine, "ray", [(i, (i + d) % 4) for i in range(4)])
        total = total + got.astype(F32)
    ray_color = color[0:3, 0:64:4].T
    return ray_color, total[None, 0:256], total[None, 256:512], total[512:516].T[None]


def solution(mesh):
    in_specs = (
        P(("ray", "region"), None, None),
        P(("ray", "region"), None),
        P("region", None, None),
        P("region", None, None),
        P("region", None, None),
        P(("ray", "region"), None),
        P(("ray", "region"), None),
        P(("ray", "region"), None),
        P(),
    )
    out_specs = (
        P(("ray", "region"), None),
        P("region", None, None),
        P("region", None, None),
        P("region", None, None),
    )
    return jax.shard_map(local, mesh=mesh, in_specs=in_specs, out_specs=out_specs, check_vma=False)
```

```python
import functools

import jax
import jax.numpy as jnp
from jax import lax
from jax.experimental import pallas as pl
from jax.experimental.pallas import tpu as pltpu
from jax.sharding import PartitionSpec as P

F32, BF16, I32 = jnp.float32, jnp.bfloat16, jnp.int32
G = 4
NS = 16
NP = 64
ROWS = 528
MIB = 1024 * 1024
HI = lax.Precision.HIGHEST

OUT_TREE = (
    ((0, 1), (0, 0), "x", 1),
    ((1, 0), (0, 0), "z", 1),
    ((0, 3), (0, 0), "x", 3),
    ((3, 0), (0, 0), "z", 3),
    ((0, 2), (0, 1), "x", 1),
    ((2, 0), (3, 0), "z", 3),
    ((1, 1), (1, 0), "x", 1),
    ((3, 1), (0, 1), "z", 3),
    ((3, 3), (3, 0), "x", 3),
    ((1, 3), (0, 3), "z", 1),
    ((1, 2), (0, 2), "z", 1),
    ((2, 1), (2, 0), "x", 1),
    ((3, 2), (0, 2), "z", 3),
    ((2, 3), (2, 0), "x", 3),
    ((2, 2), (2, 0), "x", 2),
)
BACK_TREE = (
    ((2, 2), (2, 0), "x", 2),
    ((1, 3), (0, 3), "z", 1),
    ((3, 3), (3, 0), "x", 3),
    ((3, 1), (0, 1), "z", 3),
    ((1, 1), (1, 0), "x", 1),
    ((2, 3), (2, 0), "x", 3),
    ((3, 2), (0, 2), "z", 3),
    ((2, 1), (2, 0), "x", 1),
    ((1, 2), (0, 2), "z", 1),
    ((3, 0), (0, 0), "z", 3),
    ((0, 3), (0, 0), "x", 3),
    ((1, 0), (0, 0), "z", 1),
    ((0, 1), (0, 0), "x", 1),
    ((2, 0), (0, 0), "z", 2),
    ((0, 2), (0, 0), "x", 2),
)


def move(axis, step):
    pairs = []
    for z in range(4):
        for x in range(4):
            for c in range(2):
                z2, x2, c2 = z, x, c
                if axis == "z":
                    z2 = (z + step) % 4
                elif axis == "x":
                    x2 = (x + step) % 4
                else:
                    c2 = 1 - c
                pairs.append((z * 8 + x * 2 + c, z2 * 8 + x2 * 2 + c2))
    return pairs


def iota(shape, dim):
    return lax.broadcasted_iota(I32, shape, dim)


def meta_kernel(owner, region, order, target, delta, out):
    me = lax.axis_index("region")
    spot = region[...]
    slot = jnp.zeros((1, 64), I32)
    for r in range(32):
        slot = jnp.where(spot == r, owner[r], slot)
    dz = ((slot >> 3) - (me >> 3)) & 3
    dx = (((slot >> 1) & 3) - ((me >> 1) & 3)) & 3
    key = (dz * 4 + dx) * 2 + (slot & 1)
    rows = jnp.concatenate([order[...].astype(F32), target[...], jnp.zeros((1, 16), F32)], 0)
    ray = jnp.where((iota((16, 64), 1) >> 2) == iota((16, 64), 0), 1.0, 0.0)
    spread = jnp.dot(rows, ray, precision=HI, preferred_element_type=F32)
    pick = (iota((8, 64), 1) & 3) == iota((8, 64), 0)
    place = jnp.sum(jnp.where(pick, spread, 0.0), 0, keepdims=True)
    top = jnp.concatenate([key.astype(F32), place, spread[4:7], jnp.zeros((3, 64), F32)], 0)
    out[0:8, :] = jnp.concatenate([top, jnp.zeros((8, 64), F32)], 1)
    out[8:72, :] = delta[...].astype(F32)


def both(a, b):
    lane = iota(a.shape, 1)
    return jnp.where(lane < 64, a, pltpu.roll(b, 64, 1))


def plan_kernel(own, sib, x_own, x_sib, table, info, xa, sems):
    copies = []
    for k in range(8):
        src = (x_own, x_sib)[k // 4].at[pl.ds(k % 4 * 16, 16)]
        copies.append(pltpu.make_async_copy(src, xa.at[pl.ds(k * 16, 16)], sems.at[k]))
        copies[k].start()
    meta = both(own[0:8], sib[0:8])
    key = meta[0:1].astype(I32)
    rel, valid = key >> 1, (key & 1) == (lax.axis_index("region") & 1)
    hot = (iota((NS, 128), 0) == rel) & valid
    hotf = jnp.where(hot, 1.0, 0.0)
    before = jnp.where(iota((128, 128), 0) < iota((128, 128), 1), 1.0, 0.0)
    cum = jnp.dot(hotf, before, preferred_element_type=F32)
    rank = jnp.sum(hotf * cum, 0, keepdims=True).astype(I32)
    count = jnp.sum(hotf, 1, keepdims=True).astype(I32)
    pairs = ((count + 1) >> 1).astype(F32)
    eye = iota((NS, 128), 0) == iota((NS, 128), 1)
    pairs_row = jnp.sum(jnp.where(eye, pairs, 0.0), 0, keepdims=True)
    ahead = iota((NS, 128), 1) < iota((NS, 128), 0)
    start = jnp.sum(jnp.where(ahead, pairs_row, 0.0), 1, keepdims=True)
    start_row = jnp.sum(jnp.where(eye, start, 0.0), 0, keepdims=True)
    start_j = jnp.sum(hotf * start, 0, keepdims=True).astype(I32)
    code = start_j + (rank >> 1) + (rank & 1) * NP
    code = jnp.where(valid, code, -1)
    square = iota((128, 128), 0) == iota((128, 128), 1)
    code_col = jnp.sum(jnp.where(square, code.astype(F32), 0.0), 1, keepdims=True)
    source = (iota((128, 128), 0) + 1).astype(F32)
    hit = code_col.astype(I32) == iota((128, 128), 1)
    inverse = jnp.sum(jnp.where(hit, source, 0.0), 0, keepdims=True).astype(I32)
    inverse = jnp.maximum(inverse - 1, 0)
    begun = jnp.where(start.astype(I32) <= iota((NS, 128), 1), 1.0, 0.0)
    slot_of = jnp.sum(begun, 0, keepdims=True).astype(I32) - 1
    total = jnp.sum(pairs_row, 1, keepdims=True).astype(I32)
    table[...] = jnp.concatenate(
        [
            inverse,
            slot_of,
            start_row.astype(I32),
            pairs_row.astype(I32),
            jnp.broadcast_to(total, (1, 128)),
            jnp.zeros((3, 128), I32),
        ],
        0,
    )
    info[0:8, :] = meta
    info[8:16, :] = jnp.broadcast_to(code, (8, 128)).astype(F32)
    info[16:80, :] = own[8:72]
    info[80:144, :] = sib[8:72]
    for copy in copies:
        copy.wait()


def samples(table, xa, i):
    return jnp.concatenate([xa[table[0, i]], xa[table[0, NP + i]]], 0)


def forward_kernel(*refs):
    table, info, xa = refs[:3]
    weights = refs[3 : 3 + NS]
    res, saved, wv, h1, h2 = refs[3 + NS : 8 + NS]
    raw, wsem = refs[8 + NS :]
    groups = (table[4, 0] + G - 1) // G
    for s in range(NS):
        pltpu.make_async_copy(weights[s], wv.at[s], wsem.at[s]).start()
    raw[...] = jnp.zeros(raw.shape, F32)

    def held(s, _):
        pltpu.make_async_copy(weights[0], wv.at[s], wsem.at[s]).wait()
        return 0

    def step(t, ready):
        ids = [G * t + g for g in range(G)]
        slots = [table[1, i] for i in ids]
        lax.fori_loop(ready, slots[-1] + 1, held, 0)
        pre = [
            jnp.dot(samples(table, xa, i), wv[s, 0:256], preferred_element_type=F32)
            for i, s in zip(ids, slots)
        ]
        one = [jnp.maximum(p, 0.0).astype(BF16) for p in pre]
        pre = [
            jnp.dot(o, wv[s, 256:512], preferred_element_type=F32) for o, s in zip(one, slots)
        ]
        two = [jnp.maximum(p, 0.0).astype(BF16) for p in pre]
        out = [
            lax.dot_general(
                wv[s, 512:528], o, (((1,), (1,)), ((), ())), preferred_element_type=F32
            )
            for o, s in zip(two, slots)
        ]
        for g, i in enumerate(ids):
            h1[i] = one[g]
            h2[i] = two[g]
            rows = pl.ds(pl.multiple_of(i * 8, 8), 8)
            raw[0, rows, :] = out[g][0:8, 0:128]
            raw[1, rows, :] = out[g][0:8, 128:256]
        return slots[-1] + 1

    lax.fori_loop(lax.fori_loop(0, groups, step, 0), NS, held, 0)

    before = jnp.where(iota((128, 128), 0) < iota((128, 128), 1), 1.0, 0.0)
    spot = info[8:9].astype(I32)
    out = jnp.zeros((4, 128), F32)
    for h in range(2):
        lanes = slice(h * 128, h * 128 + 128)
        pick = spot == iota((NP, 128), 0) + h * NP
        pickb = jnp.where(pick, 1.0, 0.0).astype(BF16)
        deltas = info[16:144].astype(BF16)
        delta = jnp.dot(pickb, deltas, preferred_element_type=F32)
        ch = [raw[h, pl.ds(c, NP, stride=8), :] for c in range(4)]
        sigma = jnp.maximum(ch[0], 0.0) + jnp.log1p(jnp.exp(-jnp.abs(ch[0])))
        rgb = [jax.nn.sigmoid(ch[c]) for c in (1, 2, 3)]
        tau = sigma * delta
        cum = jnp.dot(tau, before, precision=HI, preferred_element_type=F32)
        trans = jnp.exp(-cum)
        opacity = 1.0 - jnp.exp(-tau)
        weight = trans * opacity
        cols = [jnp.sum(weight * rgb[c], 1, keepdims=True) for c in range(3)]
        cols.append(-jnp.sum(tau, 1, keepdims=True))
        out += jnp.concatenate(
            [jnp.sum(jnp.where(pick, col, 0.0), 0, keepdims=True) for col in cols], 0
        )
        keep = rgb + [weight, trans * (1.0 - opacity), delta * jax.nn.sigmoid(ch[0])]
        for k in range(6):
            saved[k, :, lanes] = keep[k]
    res[...] = jnp.concatenate([out, jnp.zeros((4, 128), F32)], 0)


def backward_kernel(*refs):
    table, info, res, res_sib, xa, saved, wv, h1, h2, color_out = refs[:10]
    grads = refs[10 : 10 + NS]
    dr, acc1, acc2, acc3 = refs[10 + NS :]
    groups = (table[4, 0] + G - 1) // G

    meta = info[0:8]
    parts = res[...] + pltpu.roll(res_sib[...], 64, 1)
    order = meta[1:2]
    square = (128, 128)
    same = (iota(square, 0) >> 2) == (iota(square, 1) >> 2)
    samef = jnp.where(same, 1.0, 0.0)
    eye = iota(square, 0) == iota(square, 1)
    order_col = jnp.sum(jnp.where(eye, order, 0.0), 1, keepdims=True)
    prior = jnp.where(same & (order_col < order), 1.0, 0.0)
    later = jnp.where(same & (order_col > order), 1.0, 0.0)
    ahead = jnp.dot(parts, prior, precision=HI, preferred_element_type=F32)[3:4]
    reach = jnp.exp(ahead)
    shown = parts * reach
    color = jnp.dot(shown, samef, precision=HI, preferred_element_type=F32)
    color_out[...] = color
    gray = color[0:3] - meta[2:5]
    portion = jnp.sum(shown[0:3] * gray, 0, keepdims=True)
    log_cot = jnp.dot(
        jnp.broadcast_to(portion, (8, 128)), later, precision=HI, preferred_element_type=F32
    )[0:1]
    cot = [reach * gray[c : c + 1] for c in range(3)] + [log_cot]

    after = jnp.where(iota(square, 0) > iota(square, 1), 1.0, 0.0)
    spot = info[8:9].astype(I32)
    dr[...] = jnp.zeros(dr.shape, F32)
    for h in range(2):
        lanes = slice(h * 128, h * 128 + 128)
        pick = spot == iota((NP, 128), 0) + h * NP
        col = [jnp.sum(jnp.where(pick, row, 0.0), 1, keepdims=True) for row in cot]
        rgb = [saved[c, :, lanes] for c in range(3)]
        weight = saved[3, :, lanes]
        d_weight = rgb[0] * col[0] + rgb[1] * col[1] + rgb[2] * col[2]
        follow = jnp.dot(d_weight * weight, after, precision=HI, preferred_element_type=F32)
        d_tau = d_weight * saved[4, :, lanes] - col[3] - follow
        dr[h, pl.ds(0, NP, stride=8), :] = d_tau * saved[5, :, lanes]
        for c in range(3):
            d_col = weight * col[c] * rgb[c] * (1.0 - rgb[c])
            dr[h, pl.ds(c + 1, NP, stride=8), :] = d_col

    for s in range(NS):

        @pl.when(table[3, s] == 0)
        def _():
            grads[s][...] = jnp.zeros((ROWS, 256), BF16)

    def step(t, _):
        ids = [G * t + g for g in range(G)]
        slots = [table[1, i] for i in ids]
        tn, nt = (((0,), (0,)), ((), ())), (((1,), (1,)), ((), ()))
        raws = []
        for i in ids:
            rows = pl.ds(pl.multiple_of(i * 8, 8), 8)
            d_raw = jnp.concatenate([dr[0, rows, :], dr[1, rows, :]], 1)
            raws.append(jnp.concatenate([d_raw, jnp.zeros((8, 256), F32)], 0).astype(BF16))
        two = [h2[i] for i in ids]
        dh = [
            lax.dot_general(r, wv[s, 512:528], tn, preferred_element_type=F32)
            for r, s in zip(raws, slots)
        ]
        d_two = [jnp.where(h > 0, d, 0.0).astype(BF16) for h, d in zip(two, dh)]
        one = [h1[i] for i in ids]
        dh = [
            lax.dot_general(d, wv[s, 256:512], nt, preferred_element_type=F32)
            for d, s in zip(d_two, slots)
        ]
        g3 = [jnp.dot(r, h, preferred_element_type=F32) for r, h in zip(raws, two)]
        g2 = [
            lax.dot_general(h, d, tn, preferred_element_type=F32) for h, d in zip(one, d_two)
        ]
        d_one = [jnp.where(h > 0, d, 0.0).astype(BF16) for h, d in zip(one, dh)]
        g1 = [
            lax.dot_general(samples(table, xa, i), d, tn, preferred_element_type=F32)
            for i, d in zip(ids, d_one)
        ]
        for g, s in enumerate(slots):
            first = ids[g] == table[2, s]
            acc1[s] = jnp.where(first, 0.0, acc1[s]) + g1[g]
            acc2[s] = jnp.where(first, 0.0, acc2[s]) + g2[g]
            acc3[s] = jnp.where(first, 0.0, acc3[s]) + g3[g]
        return 0

    lax.fori_loop(0, groups, step, 0)
    for s in range(NS):

        @pl.when(table[3, s] > 0)
        def _():
            grads[s][0:256] = acc1[s].astype(BF16)
            grads[s][256:512] = acc2[s].astype(BF16)
            grads[s][512:528] = acc3[s].astype(BF16)


def spec(space):
    return pl.BlockSpec(memory_space=space)


def local(
    features, deltas, weight_one, weight_two, weight_out, target, block_region, seg_order, owner_map
):
    smem, vmem, hbm = spec(pltpu.SMEM), spec(pltpu.VMEM), spec(pl.ANY)
    far = spec(pltpu.MemorySpace.HBM)
    shape = jax.ShapeDtypeStruct
    dma = pltpu.SemaphoreType.DMA
    limit = pltpu.CompilerParams(vmem_limit_bytes=15 * MIB)

    def away(a):
        return pltpu.with_memory_space_constraint(a, pltpu.MemorySpace.HBM)

    def swap(a):
        return lax.ppermute(a, "region", move("core", 1))

    head = jnp.pad(weight_out[0].T, ((0, 12), (0, 0)))
    held = {(0, 0): jnp.concatenate([weight_one[0], weight_two[0], head], 0)}
    x_sib = swap(features)
    for key, source, axis, step in OUT_TREE[:4]:
        held[key] = lax.ppermute(held[source], "region", move(axis, -step))
    keys = list(held)
    x_sib, *values = lax.optimization_barrier((x_sib, *held.values()))
    held = dict(zip(keys, values))
    for key, source, axis, step in OUT_TREE[4:]:
        held[key] = lax.ppermute(held[source], "region", move(axis, -step))
    weights = [held[(s // 4, s % 4)] for s in range(NS)]

    meta = pl.pallas_call(
        meta_kernel,
        out_shape=shape((72, 128), F32),
        in_specs=[smem, vmem, vmem, vmem, vmem],
        out_specs=vmem,
        name="meta",
    )(owner_map, block_region.T, seg_order.T, target.T, deltas)
    meta_sib = swap(meta)
    table, info, xa = pl.pallas_call(
        plan_kernel,
        out_shape=(shape((8, 128), I32), pltpu.VMEM((144, 128), F32), pltpu.VMEM((128, 128, 256), BF16)),
        in_specs=[vmem, vmem, far, hbm],
        out_specs=(vmem,) * 3,
        scratch_shapes=[dma((8,))],
        compiler_params=limit,
        name="plan",
    )(meta, meta_sib, away(features), x_sib)

    kept = pltpu.VMEM((NP, 256, 256), BF16)
    res, saved, wv, h1, h2 = pl.pallas_call(
        forward_kernel,
        out_shape=(
            shape((8, 128), F32),
            pltpu.VMEM((6, NP, 256), F32),
            pltpu.VMEM((NS, ROWS, 256), BF16),
            kept,
            kept,
        ),
        in_specs=[smem, vmem, vmem] + [hbm] * NS,
        out_specs=(vmem,) * 5,
        scratch_shapes=[pltpu.VMEM((2, NP * 8, 128), F32), dma((NS,))],
        compiler_params=limit,
        name="forward",
    )(table, info, xa, *weights)
    res_sib = swap(res)
    color, *grads = pl.pallas_call(
        backward_kernel,
        out_shape=(shape((8, 128), F32),) + (pltpu.VMEM((ROWS, 256), BF16),) * NS,
        in_specs=[smem] + [vmem] * 8,
        out_specs=(vmem,) * (NS + 1),
        scratch_shapes=[
            pltpu.VMEM((2, NP * 8, 128), F32),
            pltpu.VMEM((NS, 256, 256), F32),
            pltpu.VMEM((NS, 256, 256), F32),
            pltpu.VMEM((NS, 16, 256), F32),
        ],
        compiler_params=limit,
        name="backward",
    )(table, info, res, res_sib, xa, saved, wv, h1, h2)

    sums = {(s // 4, s % 4): grads[s] for s in range(NS)}
    for key, source, axis, step in BACK_TREE:
        got = lax.ppermute(sums[key], "region", move(axis, step))
        sums[source] = (sums[source].astype(F32) + got.astype(F32)).astype(BF16)
    mine = sums[(0, 0)]
    total = mine.astype(F32)
    for d in (1, 3, 2):
        got = lax.ppermute(mine, "ray", [(i, (i + d) % 4) for i in range(4)])
        total = total + got.astype(F32)
    ray_color = color[0:3, 0:64:4].T
    return ray_color, total[None, 0:256], total[None, 256:512], total[512:516].T[None]


def solution(mesh):
    in_specs = (
        P(("ray", "region"), None, None),
        P(("ray", "region"), None),
        P("region", None, None),
        P("region", None, None),
        P("region", None, None),
        P(("ray", "region"), None),
        P(("ray", "region"), None),
        P(("ray", "region"), None),
        P(),
    )
    out_specs = (
        P(("ray", "region"), None),
        P("region", None, None),
        P("region", None, None),
        P("region", None, None),
    )
    return jax.shard_map(local, mesh=mesh, in_specs=in_specs, out_specs=out_specs, check_vma=False)
```

```python
import functools

import jax
import jax.numpy as jnp
from jax import lax
from jax.experimental import pallas as pl
from jax.experimental.pallas import tpu as pltpu
from jax.sharding import PartitionSpec as P

F32, BF16, I32 = jnp.float32, jnp.bfloat16, jnp.int32
G = 4
NS = 16
NA, NB = 48, 24
NP = NA + NB
ROWS = 528
MIB = 1024 * 1024
HI = lax.Precision.HIGHEST

TREE = (
    ((0, 1), (0, 0), "x", 1),
    ((1, 0), (0, 0), "z", 1),
    ((0, 3), (0, 0), "x", 3),
    ((3, 0), (0, 0), "z", 3),
    ((0, 2), (0, 1), "x", 1),
    ((2, 0), (3, 0), "z", 3),
    ((1, 1), (1, 0), "x", 1),
    ((3, 1), (0, 1), "z", 3),
    ((3, 3), (3, 0), "x", 3),
    ((1, 3), (0, 3), "z", 1),
    ((1, 2), (0, 2), "z", 1),
    ((2, 1), (2, 0), "x", 1),
    ((3, 2), (0, 2), "z", 3),
    ((2, 3), (2, 0), "x", 3),
    ((2, 2), (2, 0), "x", 2),
)


NEAR = ((0, 0), (0, 1), (1, 0), (0, 3), (3, 0), (0, 2), (2, 0), (1, 1), (3, 1), (3, 3), (1, 3))
FAR = ((1, 2), (2, 1), (3, 2), (2, 3), (2, 2))
SLOTS = NEAR + FAR
NN, NF = len(NEAR), len(FAR)


def move(axis, step):
    pairs = []
    for z in range(4):
        for x in range(4):
            for c in range(2):
                z2, x2, c2 = z, x, c
                if axis == "z":
                    z2 = (z + step) % 4
                elif axis == "x":
                    x2 = (x + step) % 4
                else:
                    c2 = 1 - c
                pairs.append((z * 8 + x * 2 + c, z2 * 8 + x2 * 2 + c2))
    return pairs


def iota(shape, dim):
    return lax.broadcasted_iota(I32, shape, dim)


def meta_kernel(owner, region, order, target, delta, out):
    me = lax.axis_index("region")
    spot = region[...]
    slot = jnp.zeros((1, 64), I32)
    for r in range(32):
        slot = jnp.where(spot == r, owner[r], slot)
    dz = ((slot >> 3) - (me >> 3)) & 3
    dx = (((slot >> 1) & 3) - ((me >> 1) & 3)) & 3
    rel = jnp.zeros((1, 64), I32)
    for k, (a, b) in enumerate(SLOTS):
        rel = jnp.where((dz == a) & (dx == b), k, rel)
    key = rel * 2 + (slot & 1)
    rows = jnp.concatenate([order[...].astype(F32), target[...], jnp.zeros((1, 16), F32)], 0)
    ray = jnp.where((iota((16, 64), 1) >> 2) == iota((16, 64), 0), 1.0, 0.0)
    spread = jnp.dot(rows, ray, precision=HI, preferred_element_type=F32)
    pick = (iota((8, 64), 1) & 3) == iota((8, 64), 0)
    place = jnp.sum(jnp.where(pick, spread, 0.0), 0, keepdims=True)
    top = jnp.concatenate([key.astype(F32), place, spread[4:7], jnp.zeros((3, 64), F32)], 0)
    out[0:8, :] = jnp.concatenate([top, jnp.zeros((8, 64), F32)], 1)
    out[8:72, :] = delta[...].astype(F32)


def both(a, b):
    lane = iota(a.shape, 1)
    return jnp.where(lane < 64, a, pltpu.roll(b, 64, 1))


def plan_kernel(own, sib, x_own, x_sib, table, info, xa, sems):
    copies = []
    for k in range(8):
        src = (x_own, x_sib)[k // 4].at[pl.ds(k % 4 * 16, 16)]
        copies.append(pltpu.make_async_copy(src, xa.at[pl.ds(k * 16, 16)], sems.at[k]))
        copies[k].start()
    meta = both(own[0:8], sib[0:8])
    key = meta[0:1].astype(I32)
    rel, valid = key >> 1, (key & 1) == (lax.axis_index("region") & 1)
    hot = (iota((NS, 128), 0) == rel) & valid
    hotf = jnp.where(hot, 1.0, 0.0)
    before = jnp.where(iota((128, 128), 0) < iota((128, 128), 1), 1.0, 0.0)
    cum = jnp.dot(hotf, before, preferred_element_type=F32)
    rank = jnp.sum(hotf * cum, 0, keepdims=True).astype(I32)
    count = jnp.sum(hotf, 1, keepdims=True).astype(I32)
    pairs = ((count + 1) >> 1).astype(F32)
    eye = iota((NS, 128), 0) == iota((NS, 128), 1)
    pairs_row = jnp.sum(jnp.where(eye, pairs, 0.0), 0, keepdims=True)
    row, lane = iota((NS, 128), 0), iota((NS, 128), 1)
    ahead = (lane < row) & ((lane >= NN) == (row >= NN))
    start = jnp.sum(jnp.where(ahead, pairs_row, 0.0), 1, keepdims=True)
    start = start + jnp.where(row[:, 0:1] >= NN, float(NA), 0.0)
    start_row = jnp.sum(jnp.where(eye, start, 0.0), 0, keepdims=True)
    start_j = jnp.sum(hotf * start, 0, keepdims=True).astype(I32)
    code = start_j * 2 + rank
    code = jnp.where(valid, code, -1)
    square = iota((128, 128), 0) == iota((128, 128), 1)
    code_col = jnp.sum(jnp.where(square, code.astype(F32), 0.0), 1, keepdims=True)
    source = (iota((128, 128), 0) + 1).astype(F32)
    inverse = []
    for h in range(2):
        hit = code_col.astype(I32) == iota((128, 128), 1) * 2 + h
        found = jnp.sum(jnp.where(hit, source, 0.0), 0, keepdims=True).astype(I32)
        inverse.append(jnp.maximum(found - 1, 0))
    begun = jnp.where(start.astype(I32) <= iota((NS, 128), 1), 1.0, 0.0)
    slot_of = jnp.sum(begun, 0, keepdims=True).astype(I32) - 1
    near = iota((1, 128), 1) < NN
    totals = [
        jnp.sum(jnp.where(near == side, pairs_row, 0.0), 1, keepdims=True).astype(I32)
        for side in (True, False)
    ]
    table[...] = jnp.concatenate(
        [
            inverse[0],
            slot_of,
            start_row.astype(I32),
            pairs_row.astype(I32),
            jnp.broadcast_to(totals[0], (1, 128)),
            jnp.broadcast_to(totals[1], (1, 128)),
            inverse[1],
            jnp.zeros((1, 128), I32),
        ],
        0,
    )
    info[0:8, :] = meta
    info[8:16, :] = jnp.broadcast_to(code, (8, 128)).astype(F32)
    info[16:80, :] = own[8:72]
    info[80:144, :] = sib[8:72]
    for copy in copies:
        copy.wait()


def samples(table, xa, i):
    return jnp.concatenate([xa[table[0, i]], xa[table[6, i]]], 0)


def shade(table, xa, weights, wv, h1, h2, raw, wsem, first, base, total):
    count = len(weights)
    for s in range(count):
        pltpu.make_async_copy(weights[s], wv.at[s], wsem.at[s]).start()
    raw[...] = jnp.zeros(raw.shape, F32)

    def held(s, _):
        pltpu.make_async_copy(weights[0], wv.at[s], wsem.at[s]).wait()
        return 0

    def step(t, ready):
        ids = [G * t + g for g in range(G)]
        slots = [table[1, base + i] - first for i in ids]
        lax.fori_loop(ready, slots[-1] + 1, held, 0)
        pre = [
            jnp.dot(samples(table, xa, base + i), wv[s, 0:256], preferred_element_type=F32)
            for i, s in zip(ids, slots)
        ]
        one = [jnp.maximum(p, 0.0).astype(BF16) for p in pre]
        pre = [
            jnp.dot(o, wv[s, 256:512], preferred_element_type=F32) for o, s in zip(one, slots)
        ]
        two = [jnp.maximum(p, 0.0).astype(BF16) for p in pre]
        out = [
            lax.dot_general(
                wv[s, 512:528], o, (((1,), (1,)), ((), ())), preferred_element_type=F32
            )
            for o, s in zip(two, slots)
        ]
        for g, i in enumerate(ids):
            h1[i] = one[g]
            h2[i] = two[g]
            rows = pl.ds(pl.multiple_of(i * 8, 8), 8)
            raw[0, rows, :] = out[g][0:8, 0:128]
            raw[1, rows, :] = out[g][0:8, 128:256]
        return slots[-1] + 1

    done = lax.fori_loop(0, (total + G - 1) // G, step, 0)
    lax.fori_loop(done, count, held, 0)


def forward_near_kernel(*refs):
    table, xa = refs[:2]
    raw, wv, h1, h2, wsem = refs[2 + NN :]
    shade(table, xa, refs[2 : 2 + NN], wv, h1, h2, raw, wsem, 0, 0, table[4, 0])


def forward_far_kernel(*refs):
    table, info, xa, raw_near = refs[:4]
    res, saved, wv, h1, h2, raw, wsem = refs[4 + NF :]
    shade(table, xa, refs[4 : 4 + NF], wv, h1, h2, raw, wsem, NN, NA, table[5, 0])

    before = jnp.where(iota((128, 128), 0) < iota((128, 128), 1), 1.0, 0.0)
    spot = info[8:9].astype(I32)
    out = jnp.zeros((4, 128), F32)
    for h in range(2):
        lanes = slice(h * 128, h * 128 + 128)
        pick = spot == iota((NP, 128), 0) * 2 + h
        pickb = jnp.where(pick, 1.0, 0.0).astype(BF16)
        deltas = info[16:144].astype(BF16)
        delta = jnp.dot(pickb, deltas, preferred_element_type=F32)
        ch = [
            jnp.concatenate(
                [raw_near[h, pl.ds(c, NA, stride=8), :], raw[h, pl.ds(c, NB, stride=8), :]], 0
            )
            for c in range(4)
        ]
        sigma = jnp.maximum(ch[0], 0.0) + jnp.log1p(jnp.exp(-jnp.abs(ch[0])))
        rgb = [jax.nn.sigmoid(ch[c]) for c in (1, 2, 3)]
        tau = sigma * delta
        cum = jnp.dot(tau, before, precision=HI, preferred_element_type=F32)
        trans = jnp.exp(-cum)
        opacity = 1.0 - jnp.exp(-tau)
        weight = trans * opacity
        cols = [jnp.sum(weight * rgb[c], 1, keepdims=True) for c in range(3)]
        cols.append(-jnp.sum(tau, 1, keepdims=True))
        out += jnp.concatenate(
            [jnp.sum(jnp.where(pick, col, 0.0), 0, keepdims=True) for col in cols], 0
        )
        keep = rgb + [weight, trans * (1.0 - opacity), delta * jax.nn.sigmoid(ch[0])]
        for k in range(6):
            saved[k, :, lanes] = keep[k]
    res[...] = jnp.concatenate([out, jnp.zeros((4, 128), F32)], 0)


def backward_far_kernel(*refs):
    table, info, res, res_sib, xa, saved, wv, h1, h2, color_out, dr = refs[:11]
    grads = refs[11 : 11 + NF]
    accs = refs[11 + NF :]

    meta = info[0:8]
    parts = res[...] + pltpu.roll(res_sib[...], 64, 1)
    order = meta[1:2]
    square = (128, 128)
    same = (iota(square, 0) >> 2) == (iota(square, 1) >> 2)
    samef = jnp.where(same, 1.0, 0.0)
    eye = iota(square, 0) == iota(square, 1)
    order_col = jnp.sum(jnp.where(eye, order, 0.0), 1, keepdims=True)
    prior = jnp.where(same & (order_col < order), 1.0, 0.0)
    later = jnp.where(same & (order_col > order), 1.0, 0.0)
    ahead = jnp.dot(parts, prior, precision=HI, preferred_element_type=F32)[3:4]
    reach = jnp.exp(ahead)
    shown = parts * reach
    color = jnp.dot(shown, samef, precision=HI, preferred_element_type=F32)
    color_out[...] = color
    gray = color[0:3] - meta[2:5]
    portion = jnp.sum(shown[0:3] * gray, 0, keepdims=True)
    log_cot = jnp.dot(
        jnp.broadcast_to(portion, (8, 128)), later, precision=HI, preferred_element_type=F32
    )[0:1]
    cot = [reach * gray[c : c + 1] for c in range(3)] + [log_cot]

    after = jnp.where(iota(square, 0) > iota(square, 1), 1.0, 0.0)
    spot = info[8:9].astype(I32)
    dr[...] = jnp.zeros(dr.shape, F32)
    for h in range(2):
        lanes = slice(h * 128, h * 128 + 128)
        pick = spot == iota((NP, 128), 0) * 2 + h
        col = [jnp.sum(jnp.where(pick, row, 0.0), 1, keepdims=True) for row in cot]
        rgb = [saved[c, :, lanes] for c in range(3)]
        weight = saved[3, :, lanes]
        d_weight = rgb[0] * col[0] + rgb[1] * col[1] + rgb[2] * col[2]
        follow = jnp.dot(d_weight * weight, after, precision=HI, preferred_element_type=F32)
        d_tau = d_weight * saved[4, :, lanes] - col[3] - follow
        dr[h, pl.ds(0, NP, stride=8), :] = d_tau * saved[5, :, lanes]
        for c in range(3):
            d_col = weight * col[c] * rgb[c] * (1.0 - rgb[c])
            dr[h, pl.ds(c + 1, NP, stride=8), :] = d_col

    gradients(table, dr, xa, wv, h1, h2, grads, accs, NN, NA, table[5, 0])


def backward_near_kernel(*refs):
    table, dr, xa, wv, h1, h2 = refs[:6]
    grads = refs[6 : 6 + NN]
    gradients(table, dr, xa, wv, h1, h2, grads, refs[6 + NN :], 0, 0, table[4, 0])


def gradients(table, dr, xa, wv, h1, h2, grads, accs, first, base, total):
    acc1, acc2, acc3 = accs
    for s in range(len(grads)):

        @pl.when(table[3, first + s] == 0)
        def _():
            grads[s][...] = jnp.zeros((ROWS, 256), BF16)

    def step(t, _):
        ids = [G * t + g for g in range(G)]
        slots = [table[1, base + i] - first for i in ids]
        tn, nt = (((0,), (0,)), ((), ())), (((1,), (1,)), ((), ()))
        raws = []
        for i in ids:
            rows = pl.ds(pl.multiple_of((base + i) * 8, 8), 8)
            d_raw = jnp.concatenate([dr[0, rows, :], dr[1, rows, :]], 1)
            raws.append(jnp.concatenate([d_raw, jnp.zeros((8, 256), F32)], 0).astype(BF16))
        two = [h2[i] for i in ids]
        dh = [
            lax.dot_general(r, wv[s, 512:528], tn, preferred_element_type=F32)
            for r, s in zip(raws, slots)
        ]
        d_two = [jnp.where(h > 0, d, 0.0).astype(BF16) for h, d in zip(two, dh)]
        one = [h1[i] for i in ids]
        dh = [
            lax.dot_general(d, wv[s, 256:512], nt, preferred_element_type=F32)
            for d, s in zip(d_two, slots)
        ]
        g3 = [jnp.dot(r, h, preferred_element_type=F32) for r, h in zip(raws, two)]
        g2 = [
            lax.dot_general(h, d, tn, preferred_element_type=F32) for h, d in zip(one, d_two)
        ]
        d_one = [jnp.where(h > 0, d, 0.0).astype(BF16) for h, d in zip(one, dh)]
        g1 = [
            lax.dot_general(samples(table, xa, base + i), d, tn, preferred_element_type=F32)
            for i, d in zip(ids, d_one)
        ]
        for g, s in enumerate(slots):
            begins = base + ids[g] == table[2, first + s]
            acc1[s] = jnp.where(begins, 0.0, acc1[s]) + g1[g]
            acc2[s] = jnp.where(begins, 0.0, acc2[s]) + g2[g]
            acc3[s] = jnp.where(begins, 0.0, acc3[s]) + g3[g]
        return 0

    lax.fori_loop(0, (total + G - 1) // G, step, 0)
    for s in range(len(grads)):

        @pl.when(table[3, first + s] > 0)
        def _():
            grads[s][0:256] = acc1[s].astype(BF16)
            grads[s][256:512] = acc2[s].astype(BF16)
            grads[s][512:528] = acc3[s].astype(BF16)


def cost(us):
    return pl.CostEstimate(flops=int(us * 1e9), bytes_accessed=0, transcendentals=0)


def spec(space):
    return pl.BlockSpec(memory_space=space)


def local(
    features, deltas, weight_one, weight_two, weight_out, target, block_region, seg_order, owner_map
):
    smem, vmem, hbm = spec(pltpu.SMEM), spec(pltpu.VMEM), spec(pl.ANY)
    far = spec(pltpu.MemorySpace.HBM)
    shape = jax.ShapeDtypeStruct
    dma = pltpu.SemaphoreType.DMA
    limit = pltpu.CompilerParams(vmem_limit_bytes=10 * MIB)

    def away(a):
        return pltpu.with_memory_space_constraint(a, pltpu.MemorySpace.HBM)

    def swap(a):
        return lax.ppermute(a, "region", move("core", 1))

    head = jnp.pad(weight_out[0].T, ((0, 12), (0, 0)))
    held = {(0, 0): jnp.concatenate([weight_one[0], weight_two[0], head], 0)}
    x_sib = swap(features)
    for key, source, axis, step in TREE[:4]:
        held[key] = lax.ppermute(held[source], "region", move(axis, -step))
    x_sib, held[(1, 0)] = lax.optimization_barrier((x_sib, held[(1, 0)]))
    for key, source, axis, step in TREE[4:]:
        held[key] = lax.ppermute(held[source], "region", move(axis, -step))
    weights = [held[key] for key in SLOTS]

    meta = pl.pallas_call(
        meta_kernel,
        out_shape=shape((72, 128), F32),
        in_specs=[smem, vmem, vmem, vmem, vmem],
        out_specs=vmem,
        cost_estimate=cost(1.5),
        name="meta",
    )(owner_map, block_region.T, seg_order.T, target.T, deltas)
    meta_sib = swap(meta)
    table, info, xa = pl.pallas_call(
        plan_kernel,
        out_shape=(shape((8, 128), I32), pltpu.VMEM((144, 128), F32), pltpu.VMEM((128, 128, 256), BF16)),
        in_specs=[vmem, vmem, far, hbm],
        out_specs=(vmem,) * 3,
        scratch_shapes=[dma((8,))],
        compiler_params=limit,
        cost_estimate=cost(3),
        name="plan",
    )(meta, meta_sib, away(features), x_sib)

    def kept(n):
        return pltpu.VMEM((n, 256, 256), BF16)

    raw, *near = pl.pallas_call(
        forward_near_kernel,
        out_shape=(
            pltpu.VMEM((2, NA * 8, 128), F32),
            pltpu.VMEM((NN, ROWS, 256), BF16),
            kept(NA),
            kept(NA),
        ),
        in_specs=[smem, vmem] + [hbm] * NN,
        out_specs=(vmem,) * 4,
        scratch_shapes=[dma((NN,))],
        compiler_params=limit,
        cost_estimate=cost(4.5),
        name="forward_near",
    )(table, xa, *weights[:NN])
    res, saved, *far_side = pl.pallas_call(
        forward_far_kernel,
        out_shape=(
            shape((8, 128), F32),
            pltpu.VMEM((6, NP, 256), F32),
            pltpu.VMEM((NF, ROWS, 256), BF16),
            kept(NB),
            kept(NB),
        ),
        in_specs=[smem, vmem, vmem, vmem] + [hbm] * NF,
        out_specs=(vmem,) * 5,
        scratch_shapes=[pltpu.VMEM((2, NB * 8, 128), F32), dma((NF,))],
        compiler_params=limit,
        cost_estimate=cost(3),
        name="forward_far",
    )(table, info, xa, raw, *weights[NN:])
    res_sib = swap(res)
    def accs(n):
        return [
            pltpu.VMEM((n, 256, 256), F32),
            pltpu.VMEM((n, 256, 256), F32),
            pltpu.VMEM((n, 16, 256), F32),
        ]

    color, dr, *far_grads = pl.pallas_call(
        backward_far_kernel,
        out_shape=(shape((8, 128), F32), pltpu.VMEM((2, NP * 8, 128), F32))
        + (pltpu.VMEM((ROWS, 256), BF16),) * NF,
        in_specs=[smem] + [vmem] * 8,
        out_specs=(vmem,) * (NF + 2),
        scratch_shapes=accs(NF),
        compiler_params=limit,
        cost_estimate=cost(5.6),
        name="backward_far",
    )(table, info, res, res_sib, xa, saved, *far_side)
    near_grads = pl.pallas_call(
        backward_near_kernel,
        out_shape=(pltpu.VMEM((ROWS, 256), BF16),) * NN,
        in_specs=[smem] + [vmem] * 5,
        out_specs=(vmem,) * NN,
        scratch_shapes=accs(NN),
        compiler_params=limit,
        cost_estimate=cost(7.6),
        name="backward_near",
    )(table, dr, xa, *near)
    grads = list(near_grads) + far_grads

    sums = dict(zip(SLOTS, grads))
    for key, source, axis, step in reversed(TREE):
        got = lax.ppermute(sums[key], "region", move(axis, step))
        sums[source] = (sums[source].astype(F32) + got.astype(F32)).astype(BF16)
    mine = sums[(0, 0)]
    total = mine.astype(F32)
    for d in (1, 3, 2):
        got = lax.ppermute(mine, "ray", [(i, (i + d) % 4) for i in range(4)])
        total = total + got.astype(F32)
    ray_color = color[0:3, 0:64:4].T
    return ray_color, total[None, 0:256], total[None, 256:512], total[512:516].T[None]


def solution(mesh):
    in_specs = (
        P(("ray", "region"), None, None),
        P(("ray", "region"), None),
        P("region", None, None),
        P("region", None, None),
        P("region", None, None),
        P(("ray", "region"), None),
        P(("ray", "region"), None),
        P(("ray", "region"), None),
        P(),
    )
    out_specs = (
        P(("ray", "region"), None),
        P("region", None, None),
        P("region", None, None),
        P("region", None, None),
    )
    return jax.shard_map(local, mesh=mesh, in_specs=in_specs, out_specs=out_specs, check_vma=False)
```

```python
import functools

import jax
import jax.numpy as jnp
from jax import lax
from jax.experimental import pallas as pl
from jax.experimental.pallas import tpu as pltpu
from jax.sharding import PartitionSpec as P

F32, BF16, I32 = jnp.float32, jnp.bfloat16, jnp.int32
G = 4
NS = 16
NA, NB = 48, 24
NP = NA + NB
ROWS = 528
MIB = 1024 * 1024
HI = lax.Precision.HIGHEST

TREE = (
    ((0, 1), (0, 0), "x", 1),
    ((1, 0), (0, 0), "z", 1),
    ((0, 3), (0, 0), "x", 3),
    ((3, 0), (0, 0), "z", 3),
    ((0, 2), (0, 1), "x", 1),
    ((2, 0), (3, 0), "z", 3),
    ((1, 1), (1, 0), "x", 1),
    ((3, 1), (0, 1), "z", 3),
    ((3, 3), (3, 0), "x", 3),
    ((1, 3), (0, 3), "z", 1),
    ((1, 2), (0, 2), "z", 1),
    ((2, 1), (2, 0), "x", 1),
    ((3, 2), (0, 2), "z", 3),
    ((2, 3), (2, 0), "x", 3),
    ((2, 2), (2, 0), "x", 2),
)


NEAR = ((0, 0), (0, 1), (1, 0), (0, 3), (3, 0), (0, 2), (2, 0), (1, 1), (3, 1), (3, 3), (1, 3))
FAR = ((1, 2), (2, 1), (3, 2), (2, 3), (2, 2))
SLOTS = NEAR + FAR
NN, NF = len(NEAR), len(FAR)


def move(axis, step):
    pairs = []
    for z in range(4):
        for x in range(4):
            for c in range(2):
                z2, x2, c2 = z, x, c
                if axis == "z":
                    z2 = (z + step) % 4
                elif axis == "x":
                    x2 = (x + step) % 4
                else:
                    c2 = 1 - c
                pairs.append((z * 8 + x * 2 + c, z2 * 8 + x2 * 2 + c2))
    return pairs


def iota(shape, dim):
    return lax.broadcasted_iota(I32, shape, dim)


def meta_kernel(owner, region, order, target, delta, out):
    me = lax.axis_index("region")
    spot = region[...]
    slot = jnp.zeros((1, 64), I32)
    for r in range(32):
        slot = jnp.where(spot == r, owner[r], slot)
    dz = ((slot >> 3) - (me >> 3)) & 3
    dx = (((slot >> 1) & 3) - ((me >> 1) & 3)) & 3
    rel = jnp.zeros((1, 64), I32)
    for k, (a, b) in enumerate(SLOTS):
        rel = jnp.where((dz == a) & (dx == b), k, rel)
    key = rel * 2 + (slot & 1)
    rows = jnp.concatenate([order[...].astype(F32), target[...], jnp.zeros((1, 16), F32)], 0)
    ray = jnp.where((iota((16, 64), 1) >> 2) == iota((16, 64), 0), 1.0, 0.0)
    spread = jnp.dot(rows, ray, precision=HI, preferred_element_type=F32)
    pick = (iota((8, 64), 1) & 3) == iota((8, 64), 0)
    place = jnp.sum(jnp.where(pick, spread, 0.0), 0, keepdims=True)
    top = jnp.concatenate([key.astype(F32), place, spread[4:7], jnp.zeros((3, 64), F32)], 0)
    out[0:8, :] = jnp.concatenate([top, jnp.zeros((8, 64), F32)], 1)
    out[8:72, :] = delta[...].astype(F32)


def both(a, b):
    lane = iota(a.shape, 1)
    return jnp.where(lane < 64, a, pltpu.roll(b, 64, 1))


def plan_kernel(own, sib, x_own, x_sib, table, info, xa, sems):
    copies = []
    for k in range(8):
        src = (x_own, x_sib)[k // 4].at[pl.ds(k % 4 * 16, 16)]
        copies.append(pltpu.make_async_copy(src, xa.at[pl.ds(k * 16, 16)], sems.at[k]))
        copies[k].start()
    meta = both(own[0:8], sib[0:8])
    key = meta[0:1].astype(I32)
    rel, valid = key >> 1, (key & 1) == (lax.axis_index("region") & 1)
    hot = (iota((NS, 128), 0) == rel) & valid
    hotf = jnp.where(hot, 1.0, 0.0)
    before = jnp.where(iota((128, 128), 0) < iota((128, 128), 1), 1.0, 0.0)
    cum = jnp.dot(hotf, before, preferred_element_type=F32)
    rank = jnp.sum(hotf * cum, 0, keepdims=True).astype(I32)
    count = jnp.sum(hotf, 1, keepdims=True).astype(I32)
    pairs = ((count + 1) >> 1).astype(F32)
    eye = iota((NS, 128), 0) == iota((NS, 128), 1)
    pairs_row = jnp.sum(jnp.where(eye, pairs, 0.0), 0, keepdims=True)
    row, lane = iota((NS, 128), 0), iota((NS, 128), 1)
    ahead = (lane < row) & ((lane >= NN) == (row >= NN))
    start = jnp.sum(jnp.where(ahead, pairs_row, 0.0), 1, keepdims=True)
    start = start + jnp.where(row[:, 0:1] >= NN, float(NA), 0.0)
    start_row = jnp.sum(jnp.where(eye, start, 0.0), 0, keepdims=True)
    start_j = jnp.sum(hotf * start, 0, keepdims=True).astype(I32)
    code = start_j * 2 + rank
    code = jnp.where(valid, code, -1)
    square = iota((128, 128), 0) == iota((128, 128), 1)
    code_col = jnp.sum(jnp.where(square, code.astype(F32), 0.0), 1, keepdims=True)
    source = (iota((128, 128), 0) + 1).astype(F32)
    inverse = []
    for h in range(2):
        hit = code_col.astype(I32) == iota((128, 128), 1) * 2 + h
        found = jnp.sum(jnp.where(hit, source, 0.0), 0, keepdims=True).astype(I32)
        inverse.append(jnp.maximum(found - 1, 0))
    begun = jnp.where(start.astype(I32) <= iota((NS, 128), 1), 1.0, 0.0)
    slot_of = jnp.sum(begun, 0, keepdims=True).astype(I32) - 1
    near = iota((1, 128), 1) < NN
    totals = [
        jnp.sum(jnp.where(near == side, pairs_row, 0.0), 1, keepdims=True).astype(I32)
        for side in (True, False)
    ]
    table[...] = jnp.concatenate(
        [
            inverse[0],
            slot_of,
            start_row.astype(I32),
            pairs_row.astype(I32),
            jnp.broadcast_to(totals[0], (1, 128)),
            jnp.broadcast_to(totals[1], (1, 128)),
            inverse[1],
            jnp.zeros((1, 128), I32),
        ],
        0,
    )
    info[0:8, :] = meta
    info[8:16, :] = jnp.broadcast_to(code, (8, 128)).astype(F32)
    info[16:80, :] = own[8:72]
    info[80:144, :] = sib[8:72]
    for copy in copies:
        copy.wait()


def samples(table, xa, i):
    return jnp.concatenate([xa[table[0, i]], xa[table[6, i]]], 0)


def shade(table, xa, weights, wv, h1, h2, raw, wsem, first, base, total):
    count = len(weights)
    for s in range(count):
        pltpu.make_async_copy(weights[s], wv.at[s], wsem.at[s]).start()
    raw[...] = jnp.zeros(raw.shape, F32)

    def held(s, _):
        pltpu.make_async_copy(weights[0], wv.at[s], wsem.at[s]).wait()
        return 0

    def step(t, ready):
        ids = [G * t + g for g in range(G)]
        slots = [table[1, base + i] - first for i in ids]
        lax.fori_loop(ready, slots[-1] + 1, held, 0)
        pre = [
            jnp.dot(samples(table, xa, base + i), wv[s, 0:256], preferred_element_type=F32)
            for i, s in zip(ids, slots)
        ]
        one = [jnp.maximum(p, 0.0).astype(BF16) for p in pre]
        pre = [
            jnp.dot(o, wv[s, 256:512], preferred_element_type=F32) for o, s in zip(one, slots)
        ]
        two = [jnp.maximum(p, 0.0).astype(BF16) for p in pre]
        out = [
            lax.dot_general(
                wv[s, 512:528], o, (((1,), (1,)), ((), ())), preferred_element_type=F32
            )
            for o, s in zip(two, slots)
        ]
        for g, i in enumerate(ids):
            h1[i] = one[g]
            h2[i] = two[g]
            rows = pl.ds(pl.multiple_of(i * 8, 8), 8)
            raw[0, rows, :] = out[g][0:8, 0:128]
            raw[1, rows, :] = out[g][0:8, 128:256]
        return slots[-1] + 1

    done = lax.fori_loop(0, (total + G - 1) // G, step, 0)
    lax.fori_loop(done, count, held, 0)


def forward_near_kernel(*refs):
    table, xa = refs[:2]
    raw, wv, h1, h2, wsem = refs[2 + NN :]
    shade(table, xa, refs[2 : 2 + NN], wv, h1, h2, raw, wsem, 0, 0, table[4, 0])


def forward_far_kernel(*refs):
    table, info, xa, raw_near = refs[:4]
    res, saved, wv, h1, h2, raw, wsem = refs[4 + NF :]
    shade(table, xa, refs[4 : 4 + NF], wv, h1, h2, raw, wsem, NN, NA, table[5, 0])

    before = jnp.where(iota((128, 128), 0) < iota((128, 128), 1), 1.0, 0.0)
    spot = info[8:9].astype(I32)
    out = jnp.zeros((4, 128), F32)
    for h in range(2):
        lanes = slice(h * 128, h * 128 + 128)
        pick = spot == iota((NP, 128), 0) * 2 + h
        pickb = jnp.where(pick, 1.0, 0.0).astype(BF16)
        deltas = info[16:144].astype(BF16)
        delta = jnp.dot(pickb, deltas, preferred_element_type=F32)
        ch = [
            jnp.concatenate(
                [raw_near[h, pl.ds(c, NA, stride=8), :], raw[h, pl.ds(c, NB, stride=8), :]], 0
            )
            for c in range(4)
        ]
        sigma = jnp.maximum(ch[0], 0.0) + jnp.log1p(jnp.exp(-jnp.abs(ch[0])))
        rgb = [jax.nn.sigmoid(ch[c]) for c in (1, 2, 3)]
        tau = sigma * delta
        cum = jnp.dot(tau, before, precision=HI, preferred_element_type=F32)
        trans = jnp.exp(-cum)
        opacity = 1.0 - jnp.exp(-tau)
        weight = trans * opacity
        cols = [jnp.sum(weight * rgb[c], 1, keepdims=True) for c in range(3)]
        cols.append(-jnp.sum(tau, 1, keepdims=True))
        out += jnp.concatenate(
            [jnp.sum(jnp.where(pick, col, 0.0), 0, keepdims=True) for col in cols], 0
        )
        keep = rgb + [weight, trans * (1.0 - opacity), delta * jax.nn.sigmoid(ch[0])]
        for k in range(6):
            saved[k, :, lanes] = keep[k]
    res[...] = jnp.concatenate([out, jnp.zeros((4, 128), F32)], 0)


def backward_far_kernel(*refs):
    table, info, res, res_sib, xa, saved, wv, h1, h2, color_out, dr = refs[:11]
    grads = refs[11 : 11 + NF]
    accs = refs[11 + NF :]

    meta = info[0:8]
    parts = res[...] + pltpu.roll(res_sib[...], 64, 1)
    order = meta[1:2]
    square = (128, 128)
    same = (iota(square, 0) >> 2) == (iota(square, 1) >> 2)
    samef = jnp.where(same, 1.0, 0.0)
    eye = iota(square, 0) == iota(square, 1)
    order_col = jnp.sum(jnp.where(eye, order, 0.0), 1, keepdims=True)
    prior = jnp.where(same & (order_col < order), 1.0, 0.0)
    later = jnp.where(same & (order_col > order), 1.0, 0.0)
    ahead = jnp.dot(parts, prior, precision=HI, preferred_element_type=F32)[3:4]
    reach = jnp.exp(ahead)
    shown = parts * reach
    color = jnp.dot(shown, samef, precision=HI, preferred_element_type=F32)
    color_out[...] = color
    gray = color[0:3] - meta[2:5]
    portion = jnp.sum(shown[0:3] * gray, 0, keepdims=True)
    log_cot = jnp.dot(
        jnp.broadcast_to(portion, (8, 128)), later, precision=HI, preferred_element_type=F32
    )[0:1]
    cot = [reach * gray[c : c + 1] for c in range(3)] + [log_cot]

    after = jnp.where(iota(square, 0) > iota(square, 1), 1.0, 0.0)
    spot = info[8:9].astype(I32)
    dr[...] = jnp.zeros(dr.shape, F32)
    for h in range(2):
        lanes = slice(h * 128, h * 128 + 128)
        pick = spot == iota((NP, 128), 0) * 2 + h
        col = [jnp.sum(jnp.where(pick, row, 0.0), 1, keepdims=True) for row in cot]
        rgb = [saved[c, :, lanes] for c in range(3)]
        weight = saved[3, :, lanes]
        d_weight = rgb[0] * col[0] + rgb[1] * col[1] + rgb[2] * col[2]
        follow = jnp.dot(d_weight * weight, after, precision=HI, preferred_element_type=F32)
        d_tau = d_weight * saved[4, :, lanes] - col[3] - follow
        dr[h, pl.ds(0, NP, stride=8), :] = d_tau * saved[5, :, lanes]
        for c in range(3):
            d_col = weight * col[c] * rgb[c] * (1.0 - rgb[c])
            dr[h, pl.ds(c + 1, NP, stride=8), :] = d_col

    gradients(table, dr, xa, wv, h1, h2, grads, accs, NN, NA, table[5, 0])


def backward_near_kernel(*refs):
    table, dr, xa, wv, h1, h2 = refs[:6]
    grads = refs[6 : 6 + NN]
    gradients(table, dr, xa, wv, h1, h2, grads, refs[6 + NN :], 0, 0, table[4, 0])


def gradients(table, dr, xa, wv, h1, h2, grads, accs, first, base, total):
    acc1, acc2, acc3 = accs
    for s in range(len(grads)):

        @pl.when(table[3, first + s] == 0)
        def _():
            grads[s][...] = jnp.zeros((ROWS, 256), BF16)

    def step(t, _):
        ids = [G * t + g for g in range(G)]
        slots = [table[1, base + i] - first for i in ids]
        tn, nt = (((0,), (0,)), ((), ())), (((1,), (1,)), ((), ()))
        raws = []
        for i in ids:
            rows = pl.ds(pl.multiple_of((base + i) * 8, 8), 8)
            d_raw = jnp.concatenate([dr[0, rows, :], dr[1, rows, :]], 1)
            raws.append(jnp.concatenate([d_raw, jnp.zeros((8, 256), F32)], 0).astype(BF16))
        two = [h2[i] for i in ids]
        dh = [
            lax.dot_general(r, wv[s, 512:528], tn, preferred_element_type=F32)
            for r, s in zip(raws, slots)
        ]
        d_two = [jnp.where(h > 0, d, 0.0).astype(BF16) for h, d in zip(two, dh)]
        one = [h1[i] for i in ids]
        dh = [
            lax.dot_general(d, wv[s, 256:512], nt, preferred_element_type=F32)
            for d, s in zip(d_two, slots)
        ]
        g3 = [jnp.dot(r, h, preferred_element_type=F32) for r, h in zip(raws, two)]
        g2 = [
            lax.dot_general(h, d, tn, preferred_element_type=F32) for h, d in zip(one, d_two)
        ]
        d_one = [jnp.where(h > 0, d, 0.0).astype(BF16) for h, d in zip(one, dh)]
        g1 = [
            lax.dot_general(samples(table, xa, base + i), d, tn, preferred_element_type=F32)
            for i, d in zip(ids, d_one)
        ]
        for g, s in enumerate(slots):
            begins = base + ids[g] == table[2, first + s]
            acc1[s] = jnp.where(begins, 0.0, acc1[s]) + g1[g]
            acc2[s] = jnp.where(begins, 0.0, acc2[s]) + g2[g]
            acc3[s] = jnp.where(begins, 0.0, acc3[s]) + g3[g]
        return 0

    lax.fori_loop(0, (total + G - 1) // G, step, 0)
    for s in range(len(grads)):

        @pl.when(table[3, first + s] > 0)
        def _():
            grads[s][0:256] = acc1[s].astype(BF16)
            grads[s][256:512] = acc2[s].astype(BF16)
            grads[s][512:528] = acc3[s].astype(BF16)


def cost(us):
    return pl.CostEstimate(flops=int(us * 1e9), bytes_accessed=0, transcendentals=0)


def spec(space):
    return pl.BlockSpec(memory_space=space)


def local(
    features, deltas, weight_one, weight_two, weight_out, target, block_region, seg_order, owner_map
):
    smem, vmem, hbm = spec(pltpu.SMEM), spec(pltpu.VMEM), spec(pl.ANY)
    far = spec(pltpu.MemorySpace.HBM)
    shape = jax.ShapeDtypeStruct
    dma = pltpu.SemaphoreType.DMA
    limit = pltpu.CompilerParams(vmem_limit_bytes=10 * MIB)

    def away(a):
        return pltpu.with_memory_space_constraint(a, pltpu.MemorySpace.HBM)

    def swap(a):
        return lax.ppermute(a, "region", move("core", 1))

    head = jnp.pad(weight_out[0].T, ((0, 12), (0, 0)))
    held = {(0, 0): jnp.concatenate([weight_one[0], weight_two[0], head], 0)}
    x_sib = swap(features)
    for key, source, axis, step in TREE[:4]:
        held[key] = lax.ppermute(held[source], "region", move(axis, -step))
    x_sib, held[(1, 0)] = lax.optimization_barrier((x_sib, held[(1, 0)]))
    for key, source, axis, step in TREE[4:]:
        held[key] = lax.ppermute(held[source], "region", move(axis, -step))
    weights = [held[key] for key in SLOTS]

    meta = pl.pallas_call(
        meta_kernel,
        out_shape=shape((72, 128), F32),
        in_specs=[smem, vmem, vmem, vmem, vmem],
        out_specs=vmem,
        cost_estimate=cost(1.5),
        name="meta",
    )(owner_map, block_region.T, seg_order.T, target.T, deltas)
    meta_sib = swap(meta)
    table, info, xa = pl.pallas_call(
        plan_kernel,
        out_shape=(shape((8, 128), I32), pltpu.VMEM((144, 128), F32), pltpu.VMEM((128, 128, 256), BF16)),
        in_specs=[vmem, vmem, far, hbm],
        out_specs=(vmem,) * 3,
        scratch_shapes=[dma((8,))],
        compiler_params=limit,
        cost_estimate=cost(3),
        name="plan",
    )(meta, meta_sib, away(features), x_sib)

    def kept(n):
        return pltpu.VMEM((n, 256, 256), BF16)

    raw, *near = pl.pallas_call(
        forward_near_kernel,
        out_shape=(
            pltpu.VMEM((2, NA * 8, 128), F32),
            pltpu.VMEM((NN, ROWS, 256), BF16),
            kept(NA),
            kept(NA),
        ),
        in_specs=[smem, vmem] + [hbm] * NN,
        out_specs=(vmem,) * 4,
        scratch_shapes=[dma((NN,))],
        compiler_params=limit,
        cost_estimate=cost(4.5),
        name="forward_near",
    )(table, xa, *weights[:NN])
    res, saved, *far_side = pl.pallas_call(
        forward_far_kernel,
        out_shape=(
            shape((8, 128), F32),
            pltpu.VMEM((6, NP, 256), F32),
            pltpu.VMEM((NF, ROWS, 256), BF16),
            kept(NB),
            kept(NB),
        ),
        in_specs=[smem, vmem, vmem, vmem] + [hbm] * NF,
        out_specs=(vmem,) * 5,
        scratch_shapes=[pltpu.VMEM((2, NB * 8, 128), F32), dma((NF,))],
        compiler_params=limit,
        cost_estimate=cost(3),
        name="forward_far",
    )(table, info, xa, raw, *weights[NN:])
    res_sib = swap(res)
    def accs(n):
        return [
            pltpu.VMEM((n, 256, 256), F32),
            pltpu.VMEM((n, 256, 256), F32),
            pltpu.VMEM((n, 16, 256), F32),
        ]

    color, dr, *far_grads = pl.pallas_call(
        backward_far_kernel,
        out_shape=(shape((8, 128), F32), pltpu.VMEM((2, NP * 8, 128), F32))
        + (pltpu.VMEM((ROWS, 256), BF16),) * NF,
        in_specs=[smem] + [vmem] * 8,
        out_specs=(vmem,) * (NF + 2),
        scratch_shapes=accs(NF),
        compiler_params=limit,
        cost_estimate=cost(5.6),
        name="backward_far",
    )(table, info, res, res_sib, xa, saved, *far_side)
    near_grads = pl.pallas_call(
        backward_near_kernel,
        out_shape=(pltpu.VMEM((ROWS, 256), BF16),) * NN,
        in_specs=[smem] + [vmem] * 5,
        out_specs=(vmem,) * NN,
        scratch_shapes=accs(NN),
        compiler_params=limit,
        cost_estimate=cost(7.6),
        name="backward_near",
    )(table, dr, xa, *near)
    grads = list(near_grads) + far_grads

    sums = dict(zip(SLOTS, grads))
    for key, source, axis, step in reversed(TREE):
        got = lax.ppermute(sums[key], "region", move(axis, step))
        sums[source] = (sums[source].astype(F32) + got.astype(F32)).astype(BF16)
    mine = sums[(0, 0)]
    parts = [mine]
    for d in (1, 3, 2):
        parts.append(lax.ppermute(mine, "ray", [(i, (i + d) % 4) for i in range(4)]))

    def ray_sum(rows):
        first, *others = [part[rows].astype(F32) for part in parts]
        for other in others:
            first = first + other
        return first

    ray_color = color[0:3, 0:64:4].T
    grad_out = ray_sum(slice(512, 516)).T
    return ray_color, ray_sum(slice(0, 256))[None], ray_sum(slice(256, 512))[None], grad_out[None]


def solution(mesh):
    in_specs = (
        P(("ray", "region"), None, None),
        P(("ray", "region"), None),
        P("region", None, None),
        P("region", None, None),
        P("region", None, None),
        P(("ray", "region"), None),
        P(("ray", "region"), None),
        P(("ray", "region"), None),
        P(),
    )
    out_specs = (
        P(("ray", "region"), None),
        P("region", None, None),
        P("region", None, None),
        P("region", None, None),
    )
    return jax.shard_map(local, mesh=mesh, in_specs=in_specs, out_specs=out_specs, check_vma=False)
```

```python
import functools

import jax
import jax.numpy as jnp
from jax import lax
from jax.experimental import pallas as pl
from jax.experimental.pallas import tpu as pltpu
from jax.sharding import PartitionSpec as P

F32, BF16, I32 = jnp.float32, jnp.bfloat16, jnp.int32
G = 4
NS = 16
NA, NB = 48, 24
NP = NA + NB
ROWS = 528
MIB = 1024 * 1024
HI = lax.Precision.HIGHEST

TREE = (
    ((0, 1), (0, 0), "x", 1),
    ((1, 0), (0, 0), "z", 1),
    ((0, 3), (0, 0), "x", 3),
    ((3, 0), (0, 0), "z", 3),
    ((0, 2), (0, 1), "x", 1),
    ((2, 0), (3, 0), "z", 3),
    ((1, 1), (1, 0), "x", 1),
    ((3, 1), (0, 1), "z", 3),
    ((3, 3), (3, 0), "x", 3),
    ((1, 3), (0, 3), "z", 1),
    ((1, 2), (0, 2), "z", 1),
    ((2, 1), (2, 0), "x", 1),
    ((3, 2), (0, 2), "z", 3),
    ((2, 3), (2, 0), "x", 3),
    ((2, 2), (2, 0), "x", 2),
)


NEAR = ((0, 0), (0, 1), (1, 0), (0, 3), (3, 0), (0, 2), (2, 0), (1, 1), (3, 1), (3, 3), (1, 3))
FAR = ((1, 2), (2, 1), (3, 2), (2, 3), (2, 2))
SLOTS = NEAR + FAR
NN, NF, NT = len(NEAR), len(FAR), 7


def move(axis, step):
    pairs = []
    for z in range(4):
        for x in range(4):
            for c in range(2):
                z2, x2, c2 = z, x, c
                if axis == "z":
                    z2 = (z + step) % 4
                elif axis == "x":
                    x2 = (x + step) % 4
                else:
                    c2 = 1 - c
                pairs.append((z * 8 + x * 2 + c, z2 * 8 + x2 * 2 + c2))
    return pairs


def iota(shape, dim):
    return lax.broadcasted_iota(I32, shape, dim)


def meta_kernel(owner, region, order, target, delta, out):
    me = lax.axis_index("region")
    spot = region[...]
    slot = jnp.zeros((1, 64), I32)
    for r in range(32):
        slot = jnp.where(spot == r, owner[r], slot)
    dz = ((slot >> 3) - (me >> 3)) & 3
    dx = (((slot >> 1) & 3) - ((me >> 1) & 3)) & 3
    rel = jnp.zeros((1, 64), I32)
    for k, (a, b) in enumerate(SLOTS):
        rel = jnp.where((dz == a) & (dx == b), k, rel)
    key = rel * 2 + (slot & 1)
    rows = jnp.concatenate([order[...].astype(F32), target[...], jnp.zeros((1, 16), F32)], 0)
    ray = jnp.where((iota((16, 64), 1) >> 2) == iota((16, 64), 0), 1.0, 0.0)
    spread = jnp.dot(rows, ray, precision=HI, preferred_element_type=F32)
    pick = (iota((8, 64), 1) & 3) == iota((8, 64), 0)
    place = jnp.sum(jnp.where(pick, spread, 0.0), 0, keepdims=True)
    top = jnp.concatenate([key.astype(F32), place, spread[4:7], jnp.zeros((3, 64), F32)], 0)
    out[0:8, :] = jnp.concatenate([top, jnp.zeros((8, 64), F32)], 1)
    out[8:72, :] = delta[...].astype(F32)


def both(a, b):
    lane = iota(a.shape, 1)
    return jnp.where(lane < 64, a, pltpu.roll(b, 64, 1))


def plan_kernel(own, sib, x_own, x_sib, table, info, xa, sems):
    copies = []
    for k in range(8):
        src = (x_own, x_sib)[k // 4].at[pl.ds(k % 4 * 16, 16)]
        copies.append(pltpu.make_async_copy(src, xa.at[pl.ds(k * 16, 16)], sems.at[k]))
        copies[k].start()
    meta = both(own[0:8], sib[0:8])
    key = meta[0:1].astype(I32)
    rel, valid = key >> 1, (key & 1) == (lax.axis_index("region") & 1)
    hot = (iota((NS, 128), 0) == rel) & valid
    hotf = jnp.where(hot, 1.0, 0.0)
    before = jnp.where(iota((128, 128), 0) < iota((128, 128), 1), 1.0, 0.0)
    cum = jnp.dot(hotf, before, preferred_element_type=F32)
    rank = jnp.sum(hotf * cum, 0, keepdims=True).astype(I32)
    count = jnp.sum(hotf, 1, keepdims=True).astype(I32)
    pairs = ((count + 1) >> 1).astype(F32)
    eye = iota((NS, 128), 0) == iota((NS, 128), 1)
    pairs_row = jnp.sum(jnp.where(eye, pairs, 0.0), 0, keepdims=True)
    row, lane = iota((NS, 128), 0), iota((NS, 128), 1)
    ahead = (lane < row) & ((lane >= NN) == (row >= NN))
    start = jnp.sum(jnp.where(ahead, pairs_row, 0.0), 1, keepdims=True)
    start = start + jnp.where(row[:, 0:1] >= NN, float(NA), 0.0)
    start_row = jnp.sum(jnp.where(eye, start, 0.0), 0, keepdims=True)
    start_j = jnp.sum(hotf * start, 0, keepdims=True).astype(I32)
    code = start_j * 2 + rank
    code = jnp.where(valid, code, -1)
    square = iota((128, 128), 0) == iota((128, 128), 1)
    code_col = jnp.sum(jnp.where(square, code.astype(F32), 0.0), 1, keepdims=True)
    source = (iota((128, 128), 0) + 1).astype(F32)
    inverse = []
    for h in range(2):
        hit = code_col.astype(I32) == iota((128, 128), 1) * 2 + h
        found = jnp.sum(jnp.where(hit, source, 0.0), 0, keepdims=True).astype(I32)
        inverse.append(jnp.maximum(found - 1, 0))
    begun = jnp.where(start.astype(I32) <= iota((NS, 128), 1), 1.0, 0.0)
    slot_of = jnp.sum(begun, 0, keepdims=True).astype(I32) - 1
    near = iota((1, 128), 1) < NN
    totals = [
        jnp.sum(jnp.where(near == side, pairs_row, 0.0), 1, keepdims=True).astype(I32)
        for side in (True, False)
    ]
    table[...] = jnp.concatenate(
        [
            inverse[0],
            slot_of,
            start_row.astype(I32),
            pairs_row.astype(I32),
            jnp.broadcast_to(totals[0], (1, 128)),
            jnp.broadcast_to(totals[1], (1, 128)),
            inverse[1],
            jnp.zeros((1, 128), I32),
        ],
        0,
    )
    info[0:8, :] = meta
    info[8:16, :] = jnp.broadcast_to(code, (8, 128)).astype(F32)
    info[16:80, :] = own[8:72]
    info[80:144, :] = sib[8:72]
    for copy in copies:
        copy.wait()


def samples(table, xa, i):
    return jnp.concatenate([xa[table[0, i]], xa[table[6, i]]], 0)


def shade(table, xa, weights, wv, h1, h2, raw, wsem, first, base, total):
    count = len(weights)
    for s in range(count):
        pltpu.make_async_copy(weights[s], wv.at[s], wsem.at[s]).start()
    raw[...] = jnp.zeros(raw.shape, F32)

    def held(s, _):
        pltpu.make_async_copy(weights[0], wv.at[s], wsem.at[s]).wait()
        return 0

    def step(t, ready):
        ids = [G * t + g for g in range(G)]
        slots = [table[1, base + i] - first for i in ids]
        lax.fori_loop(ready, slots[-1] + 1, held, 0)
        pre = [
            jnp.dot(samples(table, xa, base + i), wv[s, 0:256], preferred_element_type=F32)
            for i, s in zip(ids, slots)
        ]
        one = [jnp.maximum(p, 0.0).astype(BF16) for p in pre]
        pre = [
            jnp.dot(o, wv[s, 256:512], preferred_element_type=F32) for o, s in zip(one, slots)
        ]
        two = [jnp.maximum(p, 0.0).astype(BF16) for p in pre]
        out = [
            lax.dot_general(
                wv[s, 512:528], o, (((1,), (1,)), ((), ())), preferred_element_type=F32
            )
            for o, s in zip(two, slots)
        ]
        for g, i in enumerate(ids):
            h1[i] = one[g]
            h2[i] = two[g]
            rows = pl.ds(pl.multiple_of(i * 8, 8), 8)
            raw[0, rows, :] = out[g][0:8, 0:128]
            raw[1, rows, :] = out[g][0:8, 128:256]
        return slots[-1] + 1

    done = lax.fori_loop(0, (total + G - 1) // G, step, 0)
    lax.fori_loop(done, count, held, 0)


def forward_near_kernel(*refs):
    table, xa = refs[:2]
    raw, wv, h1, h2, wsem = refs[2 + NN :]
    shade(table, xa, refs[2 : 2 + NN], wv, h1, h2, raw, wsem, 0, 0, table[4, 0])


def forward_far_kernel(*refs):
    table, info, xa, raw_near = refs[:4]
    res, saved, wv, h1, h2, raw, wsem = refs[4 + NF :]
    shade(table, xa, refs[4 : 4 + NF], wv, h1, h2, raw, wsem, NN, NA, table[5, 0])

    before = jnp.where(iota((128, 128), 0) < iota((128, 128), 1), 1.0, 0.0)
    spot = info[8:9].astype(I32)
    out = jnp.zeros((4, 128), F32)
    for h in range(2):
        lanes = slice(h * 128, h * 128 + 128)
        pick = spot == iota((NP, 128), 0) * 2 + h
        pickb = jnp.where(pick, 1.0, 0.0).astype(BF16)
        deltas = info[16:144].astype(BF16)
        delta = jnp.dot(pickb, deltas, preferred_element_type=F32)
        ch = [
            jnp.concatenate(
                [raw_near[h, pl.ds(c, NA, stride=8), :], raw[h, pl.ds(c, NB, stride=8), :]], 0
            )
            for c in range(4)
        ]
        sigma = jnp.maximum(ch[0], 0.0) + jnp.log1p(jnp.exp(-jnp.abs(ch[0])))
        rgb = [jax.nn.sigmoid(ch[c]) for c in (1, 2, 3)]
        tau = sigma * delta
        cum = jnp.dot(tau, before, precision=HI, preferred_element_type=F32)
        trans = jnp.exp(-cum)
        opacity = 1.0 - jnp.exp(-tau)
        weight = trans * opacity
        cols = [jnp.sum(weight * rgb[c], 1, keepdims=True) for c in range(3)]
        cols.append(-jnp.sum(tau, 1, keepdims=True))
        out += jnp.concatenate(
            [jnp.sum(jnp.where(pick, col, 0.0), 0, keepdims=True) for col in cols], 0
        )
        keep = rgb + [weight, trans * (1.0 - opacity), delta * jax.nn.sigmoid(ch[0])]
        for k in range(6):
            saved[k, :, lanes] = keep[k]
    res[...] = jnp.concatenate([out, jnp.zeros((4, 128), F32)], 0)


def backward_far_kernel(*refs):
    table, info, res, res_sib, xa, saved, wv, h1, h2, color_out, dr = refs[:11]
    grads = refs[11 : 11 + NF]
    accs = refs[11 + NF :]

    meta = info[0:8]
    parts = res[...] + pltpu.roll(res_sib[...], 64, 1)
    order = meta[1:2]
    square = (128, 128)
    same = (iota(square, 0) >> 2) == (iota(square, 1) >> 2)
    samef = jnp.where(same, 1.0, 0.0)
    eye = iota(square, 0) == iota(square, 1)
    order_col = jnp.sum(jnp.where(eye, order, 0.0), 1, keepdims=True)
    prior = jnp.where(same & (order_col < order), 1.0, 0.0)
    later = jnp.where(same & (order_col > order), 1.0, 0.0)
    ahead = jnp.dot(parts, prior, precision=HI, preferred_element_type=F32)[3:4]
    reach = jnp.exp(ahead)
    shown = parts * reach
    color = jnp.dot(shown, samef, precision=HI, preferred_element_type=F32)
    color_out[...] = color
    gray = color[0:3] - meta[2:5]
    portion = jnp.sum(shown[0:3] * gray, 0, keepdims=True)
    log_cot = jnp.dot(
        jnp.broadcast_to(portion, (8, 128)), later, precision=HI, preferred_element_type=F32
    )[0:1]
    cot = [reach * gray[c : c + 1] for c in range(3)] + [log_cot]

    after = jnp.where(iota(square, 0) > iota(square, 1), 1.0, 0.0)
    spot = info[8:9].astype(I32)
    dr[...] = jnp.zeros(dr.shape, F32)
    for h in range(2):
        lanes = slice(h * 128, h * 128 + 128)
        pick = spot == iota((NP, 128), 0) * 2 + h
        col = [jnp.sum(jnp.where(pick, row, 0.0), 1, keepdims=True) for row in cot]
        rgb = [saved[c, :, lanes] for c in range(3)]
        weight = saved[3, :, lanes]
        d_weight = rgb[0] * col[0] + rgb[1] * col[1] + rgb[2] * col[2]
        follow = jnp.dot(d_weight * weight, after, precision=HI, preferred_element_type=F32)
        d_tau = d_weight * saved[4, :, lanes] - col[3] - follow
        dr[h, pl.ds(0, NP, stride=8), :] = d_tau * saved[5, :, lanes]
        for c in range(3):
            d_col = weight * col[c] * rgb[c] * (1.0 - rgb[c])
            dr[h, pl.ds(c + 1, NP, stride=8), :] = d_col

    gradients(table, dr, xa, wv, h1, h2, grads, accs, NN, NA, 0, table[5, 0], 0)


def backward_leaf_kernel(*refs):
    grads, accs = refs[6 : 6 + NN - NT], refs[6 + NN - NT :]
    gradients(*refs[:6], grads, accs, 0, 0, refs[0][2, NT], refs[0][4, 0], NT)


def backward_trunk_kernel(*refs):
    grads, accs = refs[6 : 6 + NT], refs[6 + NT :]
    gradients(*refs[:6], grads, accs, 0, 0, 0, refs[0][2, NT], 0)


def gradients(table, dr, xa, wv, h1, h2, grads, accs, first, base, begin, end, low):
    acc1, acc2, acc3 = accs
    for s in range(len(grads)):

        @pl.when(table[3, first + low + s] == 0)
        def _():
            grads[s][...] = jnp.zeros((ROWS, 256), BF16)

    def step(t, _):
        ids = [begin + G * t + g for g in range(G)]
        slots = [table[1, base + i] - first for i in ids]
        tn, nt = (((0,), (0,)), ((), ())), (((1,), (1,)), ((), ()))
        raws = []
        for i in ids:
            rows = pl.ds(pl.multiple_of((base + i) * 8, 8), 8)
            d_raw = jnp.concatenate([dr[0, rows, :], dr[1, rows, :]], 1)
            raws.append(jnp.concatenate([d_raw, jnp.zeros((8, 256), F32)], 0).astype(BF16))
        two = [h2[i] for i in ids]
        dh = [
            lax.dot_general(r, wv[s, 512:528], tn, preferred_element_type=F32)
            for r, s in zip(raws, slots)
        ]
        d_two = [jnp.where(h > 0, d, 0.0).astype(BF16) for h, d in zip(two, dh)]
        one = [h1[i] for i in ids]
        dh = [
            lax.dot_general(d, wv[s, 256:512], nt, preferred_element_type=F32)
            for d, s in zip(d_two, slots)
        ]
        g3 = [jnp.dot(r, h, preferred_element_type=F32) for r, h in zip(raws, two)]
        g2 = [
            lax.dot_general(h, d, tn, preferred_element_type=F32) for h, d in zip(one, d_two)
        ]
        d_one = [jnp.where(h > 0, d, 0.0).astype(BF16) for h, d in zip(one, dh)]
        g1 = [
            lax.dot_general(samples(table, xa, base + i), d, tn, preferred_element_type=F32)
            for i, d in zip(ids, d_one)
        ]
        for g, slot in enumerate(slots):
            begins = base + ids[g] == table[2, first + slot]
            s = slot - low
            acc1[s] = jnp.where(begins, 0.0, acc1[s]) + g1[g]
            acc2[s] = jnp.where(begins, 0.0, acc2[s]) + g2[g]
            acc3[s] = jnp.where(begins, 0.0, acc3[s]) + g3[g]
        return 0

    lax.fori_loop(0, (end - begin + G - 1) // G, step, 0)
    for s in range(len(grads)):

        @pl.when(table[3, first + low + s] > 0)
        def _():
            grads[s][0:256] = acc1[s].astype(BF16)
            grads[s][256:512] = acc2[s].astype(BF16)
            grads[s][512:528] = acc3[s].astype(BF16)


def cost(us):
    return pl.CostEstimate(flops=int(us * 1e9), bytes_accessed=0, transcendentals=0)


def spec(space):
    return pl.BlockSpec(memory_space=space)


def local(
    features, deltas, weight_one, weight_two, weight_out, target, block_region, seg_order, owner_map
):
    smem, vmem, hbm = spec(pltpu.SMEM), spec(pltpu.VMEM), spec(pl.ANY)
    far = spec(pltpu.MemorySpace.HBM)
    shape = jax.ShapeDtypeStruct
    dma = pltpu.SemaphoreType.DMA
    limit = pltpu.CompilerParams(vmem_limit_bytes=10 * MIB)

    def away(a):
        return pltpu.with_memory_space_constraint(a, pltpu.MemorySpace.HBM)

    def swap(a):
        return lax.ppermute(a, "region", move("core", 1))

    head = jnp.pad(weight_out[0].T, ((0, 12), (0, 0)))
    held = {(0, 0): jnp.concatenate([weight_one[0], weight_two[0], head], 0)}
    x_sib = swap(features)
    for key, source, axis, step in TREE[:4]:
        held[key] = lax.ppermute(held[source], "region", move(axis, -step))
    x_sib, held[(1, 0)] = lax.optimization_barrier((x_sib, held[(1, 0)]))
    for key, source, axis, step in TREE[4:]:
        held[key] = lax.ppermute(held[source], "region", move(axis, -step))
    weights = [held[key] for key in SLOTS]

    meta = pl.pallas_call(
        meta_kernel,
        out_shape=shape((72, 128), F32),
        in_specs=[smem, vmem, vmem, vmem, vmem],
        out_specs=vmem,
        cost_estimate=cost(1.5),
        name="meta",
    )(owner_map, block_region.T, seg_order.T, target.T, deltas)
    meta_sib = swap(meta)
    table, info, xa = pl.pallas_call(
        plan_kernel,
        out_shape=(shape((8, 128), I32), pltpu.VMEM((144, 128), F32), pltpu.VMEM((128, 128, 256), BF16)),
        in_specs=[vmem, vmem, far, hbm],
        out_specs=(vmem,) * 3,
        scratch_shapes=[dma((8,))],
        compiler_params=limit,
        cost_estimate=cost(3),
        name="plan",
    )(meta, meta_sib, away(features), x_sib)

    def kept(n):
        return pltpu.VMEM((n, 256, 256), BF16)

    raw, *near = pl.pallas_call(
        forward_near_kernel,
        out_shape=(
            pltpu.VMEM((2, NA * 8, 128), F32),
            pltpu.VMEM((NN, ROWS, 256), BF16),
            kept(NA),
            kept(NA),
        ),
        in_specs=[smem, vmem] + [hbm] * NN,
        out_specs=(vmem,) * 4,
        scratch_shapes=[dma((NN,))],
        compiler_params=limit,
        cost_estimate=cost(4.5),
        name="forward_near",
    )(table, xa, *weights[:NN])
    res, saved, *far_side = pl.pallas_call(
        forward_far_kernel,
        out_shape=(
            shape((8, 128), F32),
            pltpu.VMEM((6, NP, 256), F32),
            pltpu.VMEM((NF, ROWS, 256), BF16),
            kept(NB),
            kept(NB),
        ),
        in_specs=[smem, vmem, vmem, vmem] + [hbm] * NF,
        out_specs=(vmem,) * 5,
        scratch_shapes=[pltpu.VMEM((2, NB * 8, 128), F32), dma((NF,))],
        compiler_params=limit,
        cost_estimate=cost(3),
        name="forward_far",
    )(table, info, xa, raw, *weights[NN:])
    res_sib = swap(res)
    def accs(n):
        return [
            pltpu.VMEM((n, 256, 256), F32),
            pltpu.VMEM((n, 256, 256), F32),
            pltpu.VMEM((n, 16, 256), F32),
        ]

    color, dr, *far_grads = pl.pallas_call(
        backward_far_kernel,
        out_shape=(shape((8, 128), F32), pltpu.VMEM((2, NP * 8, 128), F32))
        + (pltpu.VMEM((ROWS, 256), BF16),) * NF,
        in_specs=[smem] + [vmem] * 8,
        out_specs=(vmem,) * (NF + 2),
        scratch_shapes=accs(NF),
        compiler_params=limit,
        cost_estimate=cost(5.6),
        name="backward_far",
    )(table, info, res, res_sib, xa, saved, *far_side)
    leaf_grads = pl.pallas_call(
        backward_leaf_kernel,
        out_shape=(pltpu.VMEM((ROWS, 256), BF16),) * (NN - NT),
        in_specs=[smem] + [vmem] * 5,
        out_specs=(vmem,) * (NN - NT),
        scratch_shapes=accs(NN - NT),
        compiler_params=limit,
        cost_estimate=cost(3),
        name="backward_leaf",
    )(table, dr, xa, *near)
    trunk_grads = pl.pallas_call(
        backward_trunk_kernel,
        out_shape=(pltpu.VMEM((ROWS, 256), BF16),) * NT,
        in_specs=[smem] + [vmem] * 5,
        out_specs=(vmem,) * NT,
        scratch_shapes=accs(NN),
        compiler_params=limit,
        cost_estimate=cost(5),
        name="backward_trunk",
    )(table, dr, xa, *near)
    grads = list(trunk_grads) + list(leaf_grads) + far_grads

    sums = dict(zip(SLOTS, grads))
    for key, source, axis, step in reversed(TREE):
        got = lax.ppermute(sums[key], "region", move(axis, step))
        sums[source] = (sums[source].astype(F32) + got.astype(F32)).astype(BF16)
    mine = sums[(0, 0)]
    parts = [mine]
    for d in (1, 3, 2):
        parts.append(lax.ppermute(mine, "ray", [(i, (i + d) % 4) for i in range(4)]))

    def ray_sum(rows):
        first, *others = [part[rows].astype(F32) for part in parts]
        for other in others:
            first = first + other
        return first

    ray_color = color[0:3, 0:64:4].T
    grad_out = ray_sum(slice(512, 516)).T
    return ray_color, ray_sum(slice(0, 256))[None], ray_sum(slice(256, 512))[None], grad_out[None]


def solution(mesh):
    in_specs = (
        P(("ray", "region"), None, None),
        P(("ray", "region"), None),
        P("region", None, None),
        P("region", None, None),
        P("region", None, None),
        P(("ray", "region"), None),
        P(("ray", "region"), None),
        P(("ray", "region"), None),
        P(),
    )
    out_specs = (
        P(("ray", "region"), None),
        P("region", None, None),
        P("region", None, None),
        P("region", None, None),
    )
    return jax.shard_map(local, mesh=mesh, in_specs=in_specs, out_specs=out_specs, check_vma=False)
```
